32 devices in a mesh: slab: 16 (over z, y, core), sub: 2 (over x).
Axes of the slice: x: 2, y: 2, z: 4, core: 2. Of those that a mesh axis runs over, the one named last changes fastest.
Arguments:
- features: bfloat16 [32768, 128], P(('slab', 'sub')), may hold values from -6 to 6
- positions: float32 [3, 32768], P(None, ('slab', 'sub')), may hold values from 0 to 1, as said below
- atom_count: int32 [32], P(('slab', 'sub')), may hold values from 512 to 1024, as said below
- kgrid: int32 [3, 2048], replicated, may hold values from -6 to 6
- k_filter: float32 [2048, 128], replicated, may hold values from 0.1 to 1
- w_mix: float32 [128, 128], replicated, may hold values from -0.5 to 0.5
- w_recv: bfloat16 [128, 128], replicated, may hold values from -0.5 to 0.5
- w_send: bfloat16 [128, 128], replicated, may hold values from -0.5 to 0.5
- w_basis: bfloat16 [8, 128], replicated, may hold values from -2 to 2
- w_out: bfloat16 [128, 128], replicated, may hold values from -0.5 to 0.5
- edge_basis: bfloat16 [8, 1048576], P(None, ('slab', 'sub')), may hold values from -1 to 1
- senders: int32 [1048576], P(('slab', 'sub')), may hold values from 0 to 9215, as said below
Outputs:
- updated: float32 [32768, 128], P(('slab', 'sub'))
The draws below stay inside these ranges and needn't reach their ends.
Inputs may be any that keep to these rules, and one draw needn't show every extreme that they name: `atom_count`: one block has exactly 1024 live atoms; live atoms of a block are its first rows. senders[e] = (3 a + c) * 1024 + j with a, c in 0..2 and j below the atom_count of the block it names. Each atom of block (s, b) has positions[0] in [b / 2, (b + 1) / 2), positions[2] in [s / 16, (s + 1) / 16), positions[1] in [0, 1).
All inputs are finite; a program needn't handle non-finite values.
Results may differ from the reference program's by a relative error of at most 0.0021.
Values may be sent and summed in bfloat16 or wider, within the bound.
A program may use at most 128 MiB of HBM per device.

```python
import math
import jax
import jax.numpy as jnp
from jax import lax

A_DEV = 1024
C = 128
K = 2048
DEG = 32
NB = 8
SLABS = 16
COLS = 2
BLOCKS = 32
ATOMS = 32768
EDGES = 1048576


def block_counts(key):
    key = jax.random.fold_in(key, 7)
    first_key, second_key = jax.random.split(key)
    counts = jax.random.randint(first_key, (SLABS * COLS,), A_DEV // 2, A_DEV + 1)
    full_block = jax.random.randint(second_key, (), 0, SLABS * COLS)
    return (jnp.where(jnp.arange(SLABS * COLS) == full_block, A_DEV, counts).astype(jnp.int32), full_block)


def draw_atom_count(key, part):
    counts, full_block = block_counts(key)
    return counts


def draw_senders(key, part):
    counts, full_block = block_counts(key)
    key = jax.random.fold_in(key, 2)
    first_key, second_key, third_key = jax.random.split(key, 3)
    edge_slot = jnp.arange(EDGES, dtype=jnp.int32)
    block_index = edge_slot // (A_DEV * DEG)
    slab_index = block_index // COLS
    column = block_index % COLS
    slab_step = jax.random.randint(first_key, (EDGES,), 0, 3)
    col_step = jax.random.randint(second_key, (EDGES,), 0, 3)
    source = (slab_index + slab_step - 1) % SLABS * COLS + (column + col_step - 1) % COLS
    atom_index = jax.random.randint(third_key, (EDGES,), 0, counts[source])
    values = ((slab_step * 3 + col_step) * A_DEV + atom_index).astype(jnp.int32)
    full_slab = full_block // COLS
    full_col = full_block % COLS
    target = (full_slab + SLABS - 1) % SLABS * COLS + (full_col + COLS - 1) % COLS
    first_slot = target * (A_DEV * DEG)
    values = jnp.where(edge_slot == first_slot, 9 * A_DEV - 1, values)
    values = jnp.where(edge_slot == first_slot + 1, 0, values)
    return values.astype(jnp.int32)


def draw_positions(key, part):
    key = jax.random.fold_in(key, 3)
    uniform_vals = jax.random.uniform(key, (3, ATOMS), jnp.float32)
    block_index = jnp.arange(ATOMS, dtype=jnp.int32) // A_DEV
    column = (block_index % COLS).astype(jnp.float32)
    slab_index = (block_index // COLS).astype(jnp.float32)
    first_dim = (column + uniform_vals[0]) / COLS
    third_dim = (slab_index + uniform_vals[2]) / SLABS
    return jnp.stack([first_dim, uniform_vals[1], third_dim], axis=0).astype(jnp.float32)


def set_ends(values, stream_key, smallest, top_value):
    shape = values.shape
    index_at = [jax.random.randint(jax.random.fold_in(stream_key, axis), (), 0, shape[axis]) for axis in range(len(shape))]
    values = values.at[tuple(index_at)].set(smallest)
    longest = shape.index(max(shape))
    index_at[longest] = (index_at[longest] + 1) % shape[longest]
    return values.at[tuple(index_at)].set(top_value)


def block_scale(stream_key, shape, cuts, least, largest):
    level = 1.0
    for axis_at, blocks in cuts:
        draws = jax.random.uniform(jax.random.fold_in(jax.random.fold_in(stream_key, 6), axis_at), (blocks,), jnp.float32, least / len(cuts), largest / len(cuts))
        level = level * jnp.repeat(jnp.exp(draws), shape[axis_at] // blocks).reshape((-1,) + (1,) * (len(shape) - 1 - axis_at))
    return level


def bell_draw(key, dims, scale, bound, cuts=(), kind=jnp.bfloat16):
    loudness = block_scale(key, dims, cuts, -0.22, 0.18) if cuts else 1.0
    values = jax.random.normal(key, dims, jnp.float32) * scale * loudness
    return jnp.minimum(jnp.maximum(values, -bound), bound).astype(kind)


def setup_inputs(seed: int = 0) -> dict:
    key_of = jax.random.split(jax.random.key(seed), 13)
    return {
        "features": bell_draw(key_of[0], (ATOMS, C), 1.0, 6.0, ((0, 32),)),
        "positions": draw_positions(jax.random.fold_in(key_of[12], 71), 0),
        "atom_count": draw_atom_count(jax.random.fold_in(key_of[12], 71), 0),
        "kgrid": set_ends(jax.random.randint(key_of[3], (3, K), -6, 7), jax.random.fold_in(key_of[3], 1), -6, 6).astype(jnp.int32),
        "k_filter": jnp.clip(jnp.exp(jax.random.uniform(key_of[4], (K, C), jnp.float32, math.log(0.1), math.log(1.0))), 0.1, 1.0),
        "w_mix": bell_draw(key_of[5], (C, C), C ** -0.5, 0.5, (), jnp.float32),
        "w_recv": bell_draw(key_of[6], (C, C), C ** -0.5, 0.5),
        "w_send": bell_draw(key_of[7], (C, C), C ** -0.5, 0.5),
        "w_basis": bell_draw(key_of[8], (NB, C), NB ** -0.5, 2.0),
        "w_out": bell_draw(key_of[9], (C, C), C ** -0.5, 0.5),
        "edge_basis": jnp.clip(jax.random.uniform(key_of[10], (NB, EDGES), jnp.float32, -1.0, 1.0) * block_scale(key_of[10], (NB, EDGES), ((1, 32),), -0.4, 0.0), -1.0, 1.0).astype(jnp.bfloat16),
        "senders": draw_senders(jax.random.fold_in(key_of[12], 71), 0),
    }


def phase_tables(k_rows, coords):
    wave = k_rows.astype(jnp.float32)
    phase = (wave[0][:, None] * coords[0][None, :] + wave[1][:, None] * coords[1][None, :] + wave[2][:, None] * coords[2][None, :]) * (2.0 * math.pi)
    return (jnp.cos(phase).astype(jnp.bfloat16), jnp.sin(phase).astype(jnp.bfloat16))

def factor_block(k_rows, coords, masked):
    cosines, sines = phase_tables(k_rows, coords)
    return jnp.concatenate([jnp.dot(cosines, masked, preferred_element_type=jnp.float32), jnp.dot(sines, masked, preferred_element_type=jnp.float32)], axis=1)

def k_blocks(k_rows):
    k_count = k_rows.shape[1]
    k_step = 512 if k_count % 512 == 0 else k_count
    return (k_rows.reshape(3, k_count // k_step, k_step).transpose(1, 0, 2), k_step)

def factor_rows(k_rows, coords, masked):
    blocks, k_step = k_blocks(k_rows)
    parts = lax.map(lambda wave: factor_block(wave, coords, masked), blocks)
    return parts.reshape(k_rows.shape[1], parts.shape[2])

def project_block(k_rows, coords, filtered):
    cosines, sines = phase_tables(k_rows, coords)
    channels = filtered.shape[1] // 2
    contract = (((0,), (0,)), ((), ()))
    first_term = lax.dot_general(cosines, filtered[:, :channels], contract, preferred_element_type=jnp.float32)
    second_term = lax.dot_general(sines, filtered[:, channels:], contract, preferred_element_type=jnp.float32)
    return first_term + second_term

def project_rows(running, k_rows, coords, filtered):
    blocks, k_step = k_blocks(k_rows)
    pieces = filtered.reshape(blocks.shape[0], k_step, filtered.shape[1])

    def add_block(summed, operands):
        return (summed + project_block(operands[0], coords, operands[1]), None)
    result, unused = lax.scan(add_block, running, (blocks, pieces))
    return result

def filter_rows(factor_sums, k_filter, w_mix, norm_factor):
    channels = k_filter.shape[1]
    real_part = jnp.dot(factor_sums[:, :channels] * norm_factor * k_filter, w_mix, precision=lax.Precision.HIGHEST, preferred_element_type=jnp.float32)
    imag_part = jnp.dot(factor_sums[:, channels:] * norm_factor * k_filter, w_mix, precision=lax.Precision.HIGHEST, preferred_element_type=jnp.float32)
    return jnp.concatenate([real_part, imag_part], axis=1).astype(jnp.bfloat16)

def edge_messages(recv_proj, sender_pool, senders, edge_basis, w_basis, w_out, degree):
    atom_rows = recv_proj.shape[0]
    channels = recv_proj.shape[1]
    gathered = jnp.take(sender_pool, senders, axis=0).astype(jnp.float32).reshape(atom_rows, degree, channels)
    radial = lax.dot_general(edge_basis, w_basis, (((0,), (0,)), ((), ())), preferred_element_type=jnp.float32).reshape(atom_rows, degree, channels)
    hidden = jax.nn.silu(recv_proj[:, None, :] + gathered + radial).astype(jnp.bfloat16)
    message = jnp.dot(hidden.reshape(atom_rows * degree, channels), w_out, preferred_element_type=jnp.float32)
    return lax.optimization_barrier(jnp.sum(message.reshape(atom_rows, degree, channels), axis=1)) * (1.0 / math.sqrt(degree))

def reference(features, positions, atom_count, kgrid, k_filter, w_mix, w_recv, w_send, w_basis, w_out, edge_basis, senders):
    live_mask = (jnp.arange(A_DEV, dtype=jnp.int32)[None, :] < atom_count[:, None]).astype(jnp.float32)
    masked = (features.astype(jnp.float32) * live_mask.reshape(ATOMS)[:, None]).astype(jnp.bfloat16)
    coord_blocks = positions.reshape(3, BLOCKS, A_DEV).transpose(1, 0, 2)
    masked_blocks = masked.reshape(BLOCKS, A_DEV, C)

    def add_atoms(summed, operands):
        return (summed + factor_rows(kgrid, operands[0], operands[1]), None)
    factor_sums, unused = lax.scan(add_atoms, jnp.zeros((K, 2 * C), jnp.float32), (coord_blocks, masked_blocks))
    filtered = filter_rows(factor_sums, k_filter, w_mix, 1.0 / math.sqrt(ATOMS))
    send_proj = jnp.dot(features, w_send, preferred_element_type=jnp.float32).astype(jnp.bfloat16)
    recv_proj = jnp.dot(features, w_recv, preferred_element_type=jnp.float32)
    send_grid = send_proj.reshape(SLABS, COLS, A_DEV, C)
    sender_blocks = senders.reshape(BLOCKS, A_DEV * DEG)
    basis_blocks = edge_basis.reshape(NB, BLOCKS, A_DEV * DEG).transpose(1, 0, 2)
    recv_blocks = recv_proj.reshape(BLOCKS, A_DEV, C)

    def one_block(operands):
        block_index, sender_ids, basis_rows, recv_rows, coords, mask_rows = operands
        slab_index = block_index // COLS
        column = block_index % COLS
        near_slabs = (slab_index + jnp.arange(3, dtype=jnp.int32) - 1) % SLABS
        near_cols = (column + jnp.arange(3, dtype=jnp.int32) - 1) % COLS
        sender_pool = send_grid[near_slabs][:, near_cols].reshape(9 * A_DEV, C)
        aggregate = edge_messages(recv_rows, sender_pool, sender_ids, basis_rows, w_basis, w_out, DEG)
        long_range = project_rows(jnp.zeros((A_DEV, C), jnp.float32), kgrid, coords, filtered)
        return mask_rows[:, None] * (aggregate + long_range * (4.0 / math.sqrt(K)))
    updated = lax.map(one_block, (jnp.arange(BLOCKS, dtype=jnp.int32), sender_blocks, basis_blocks, recv_blocks, coord_blocks, live_mask))
    return updated.reshape(ATOMS, C)
```

```python
import math

import jax
import jax.numpy as jnp
from jax import lax
from jax.experimental import pallas as pl
from jax.experimental.pallas import tpu as pltpu
from jax.sharding import PartitionSpec as P

KMAX = 6
SIDE = 2 * KMAX + 1
PAIRS = 96
MIB = 1024 * 1024
CONTRACT_FIRST = (((0,), (0,)), ((), ()))


def table_kernel(base_cos, base_sin, masked_ref, table_ref, sums_ref, pair_cos, pair_sin):
    grid_rows = table_ref.shape[0] // 2
    channels = masked_ref.shape[1]
    atom_rows = masked_ref.shape[0]
    for a in range(KMAX + 1):
        cx, sx = base_cos[a : a + 1, :], base_sin[a : a + 1, :]
        cy, sy = base_cos[16 : 16 + SIDE, :], base_sin[16 : 16 + SIDE, :]
        pair_cos[a * SIDE : (a + 1) * SIDE, :] = cx * cy - sx * sy
        pair_sin[a * SIDE : (a + 1) * SIDE, :] = sx * cy + cx * sy
    used = (KMAX + 1) * SIDE
    pair_cos[used:, :] = jnp.zeros((PAIRS - used, atom_rows), jnp.float32)
    pair_sin[used:, :] = jnp.zeros((PAIRS - used, atom_rows), jnp.float32)

    def one_plane(q, carry):
        cz, sz = base_cos[pl.ds(32 + q, 1), :], base_sin[pl.ds(32 + q, 1), :]
        cosines = (pair_cos[...] * cz - pair_sin[...] * sz).astype(jnp.bfloat16)
        sines = (pair_sin[...] * cz + pair_cos[...] * sz).astype(jnp.bfloat16)
        at = pl.multiple_of(q * PAIRS, PAIRS)
        table_ref[pl.ds(at, PAIRS), :] = cosines
        table_ref[pl.ds(at + grid_rows, PAIRS), :] = sines
        sums_ref[pl.ds(at, PAIRS), :channels] = jnp.dot(
            cosines, masked_ref[...], preferred_element_type=jnp.float32
        )
        sums_ref[pl.ds(at, PAIRS), channels:] = jnp.dot(
            sines, masked_ref[...], preferred_element_type=jnp.float32
        )
        return carry

    lax.fori_loop(0, SIDE, one_plane, 0)
    tail = grid_rows - SIDE * PAIRS
    if tail:
        for start in (SIDE * PAIRS, grid_rows + SIDE * PAIRS):
            table_ref[start : start + tail, :] = jnp.zeros((tail, atom_rows), jnp.bfloat16)
        sums_ref[SIDE * PAIRS :, :] = jnp.zeros((tail, 2 * channels), jnp.float32)


def edge_rows(degree, group, it, snd_ref, pool, basis_ref, w_basis, recv, total):
    edges = group * degree
    first = pl.multiple_of(it * edges, edges)
    row = pl.multiple_of(it * group, group)
    radial = lax.dot_general(
        basis_ref[:, pl.ds(first, edges)],
        w_basis[...],
        CONTRACT_FIRST,
        preferred_element_type=jnp.float32,
    )
    recv_rows = recv[pl.ds(row, group), :]
    sublane = lax.broadcasted_iota(jnp.int32, pool.shape[1:], 0)
    sums = []
    for j in range(group):
        octets = []
        for octet in range(degree // 8):
            start = first + j * degree + octet * 8
            picked = pool[snd_ref[start]]
            for k in range(1, 8):
                picked = jnp.where(sublane == k, pool[snd_ref[start + k]], picked)
            octets.append(picked)
        gathered = jnp.concatenate(octets, axis=0)
        v = gathered + radial[j * degree : (j + 1) * degree, :] + recv_rows[j : j + 1, :]
        half = 0.5 * v
        hidden = (half + half * jnp.tanh(half)).astype(jnp.bfloat16)
        sums.append(jnp.sum(hidden.astype(jnp.float32), axis=0, keepdims=True))
    total[pl.ds(row, group), :] = jnp.concatenate(sums, axis=0)


def fused_kernel(
    plan,
    snd_ref,
    left_ref,
    mid_ref,
    right_ref,
    basis_ref,
    feat_ref,
    w_recv,
    w_basis,
    w_out,
    sums_ref,
    filter_ref,
    w_mix,
    agg_ref,
    factor_ref,
    pool,
    recv,
    total,
    in_plane,
    part,
    in_line,
    line_rows,
    plane_rows,
    send_a,
    recv_a,
    send_b,
    recv_b,
    send_c,
    recv_c,
    send_d,
    recv_d,
):
    degree, cols, low, members, lines, share, norm_factor = plan
    channels = feat_ref.shape[1]
    step = pl.program_id(0)
    slab, sub = lax.axis_index("slab"), lax.axis_index("sub")
    line = slab // low
    member = (slab % low) * cols + sub
    chunk = lines * share

    def plane_peer(r):
        peer = (member + r) % members
        return peer, {"slab": line * low + peer // cols, "sub": peer % cols}

    def line_peer(r):
        peer = (line + r) % lines
        return peer, {"slab": peer * low + slab % low, "sub": sub}

    def copy_a(r):
        peer, where = plane_peer(r)
        rows = pl.ds(pl.multiple_of(peer * chunk, 8), chunk)
        return pltpu.make_async_remote_copy(
            src_ref=sums_ref.at[rows],
            dst_ref=in_plane.at[r - 1],
            send_sem=send_a.at[r - 1],
            recv_sem=recv_a.at[r - 1],
            device_id=where,
            device_id_type=pl.DeviceIdType.MESH,
        )

    def copy_b(r):
        peer, where = line_peer(r)
        rows = pl.ds(pl.multiple_of(peer * share, 8), share)
        return pltpu.make_async_remote_copy(
            src_ref=part.at[rows],
            dst_ref=in_line.at[r - 1],
            send_sem=send_b.at[r - 1],
            recv_sem=recv_b.at[r - 1],
            device_id=where,
            device_id_type=pl.DeviceIdType.MESH,
        )

    def copy_c(r):
        peer, where = line_peer(r)
        return pltpu.make_async_remote_copy(
            src_ref=line_rows.at[line],
            dst_ref=line_rows.at[line],
            send_sem=send_c.at[r - 1],
            recv_sem=recv_c.at[r - 1],
            device_id=where,
            device_id_type=pl.DeviceIdType.MESH,
        )

    def copy_d(r):
        peer, where = plane_peer(r)
        return pltpu.make_async_remote_copy(
            src_ref=line_rows,
            dst_ref=plane_rows.at[member],
            send_sem=send_d.at[r - 1],
            recv_sem=recv_d.at[r - 1],
            device_id=where,
            device_id_type=pl.DeviceIdType.MESH,
        )

    def each(count, action):
        def one(r, carry):
            action(r)
            return carry

        lax.fori_loop(1, count, one, 0)

    @pl.when(step == 0)
    def _():
        barrier = pltpu.get_barrier_semaphore()

        def greet(where):
            pl.semaphore_signal(
                barrier, inc=1, device_id=where, device_id_type=pl.DeviceIdType.MESH
            )

        each(members, lambda r: greet(plane_peer(r)[1]))
        each(lines, lambda r: greet(line_peer(r)[1]))
        pl.semaphore_wait(barrier, members + lines - 2)
        each(members, lambda r: copy_a(r).start())

        blocks = left_ref.shape[0]
        for at, strip in enumerate((left_ref, mid_ref, right_ref)):

            def spread(n, carry):
                rows = strip[pl.ds(pl.multiple_of(n * 16, 16), 16), :].astype(jnp.float32)
                pool[pl.ds(at * blocks + n * 16, 16)] = jnp.broadcast_to(
                    rows[:, None, :], (16, 8, channels)
                )
                return carry

            lax.fori_loop(0, blocks // 16, spread, 0)

    @pl.when(step == 8)
    def _():
        each(members, lambda r: copy_a(r).wait_recv())
        part[...] = sums_ref[pl.ds(pl.multiple_of(member * chunk, 8), chunk), :]

        def add(r):
            part[...] += in_plane[r - 1]

        each(members, add)
        each(lines, lambda r: copy_b(r).start())

    @pl.when(step == 10)
    def _():
        each(lines, lambda r: copy_b(r).wait_recv())
        owned = part[pl.ds(pl.multiple_of(line * share, 8), share), :]
        for r in range(1, lines):
            owned = owned + in_line[r - 1]
        stacked = jnp.concatenate([owned[:, :channels], owned[:, channels:]], axis=0)
        scaled = stacked * norm_factor * filter_ref[...]
        line_rows[line] = jnp.dot(
            scaled,
            w_mix[...],
            precision=lax.Precision.HIGHEST,
            preferred_element_type=jnp.float32,
        ).astype(jnp.bfloat16)
        each(lines, lambda r: copy_c(r).start())

    @pl.when(step == 12)
    def _():
        each(lines, lambda r: copy_c(r).wait_recv())
        each(members, lambda r: copy_d(r).start())

    recv[...] = jnp.dot(feat_ref[...], w_recv[...], preferred_element_type=jnp.float32)
    atoms = feat_ref.shape[0]

    def some_atoms(it, carry):
        edge_rows(degree, 8, it, snd_ref, pool, basis_ref, w_basis, recv, total)
        return carry

    lax.fori_loop(0, atoms // 8, some_atoms, 0)
    high = total[...].astype(jnp.bfloat16)
    low_part = (total[...] - high.astype(jnp.float32)).astype(jnp.bfloat16)
    agg_ref[...] = (
        jnp.dot(high, w_out[...], preferred_element_type=jnp.float32)
        + jnp.dot(low_part, w_out[...], preferred_element_type=jnp.float32)
    ) * (1.0 / math.sqrt(degree))

    @pl.when(step == pl.num_programs(0) - 1)
    def _():
        each(members, lambda r: copy_a(r).wait_send())
        each(lines, lambda r: copy_b(r).wait_send())
        each(lines, lambda r: copy_c(r).wait_send())
        each(members, lambda r: copy_d(r).wait())
        plane_rows[member] = line_rows[...]
        grid_rows = factor_ref.shape[0] // 2

        def lay(n, carry):
            rows = plane_rows[n // lines, n % lines].astype(jnp.float32)
            factor_ref[pl.ds(pl.multiple_of(n * share, 8), share), :] = rows[:share]
            factor_ref[pl.ds(pl.multiple_of(grid_rows + n * share, 8), share), :] = rows[share:]
            return carry

        lax.fori_loop(0, members * lines, lay, 0)


def finish_kernel(scale, table_ref, factors_ref, agg_ref, mask_ref, out_ref):
    spread = lax.dot_general(
        factors_ref[...].astype(jnp.bfloat16), table_ref[...], CONTRACT_FIRST, preferred_element_type=jnp.float32
    )
    out_ref[...] = mask_ref[...] * (agg_ref[...] + spread.T * scale)


def whole(shape):
    return pl.BlockSpec(shape, lambda i: (0,) * len(shape), pipeline_mode=pl.Buffered(1))


def edges_and_factors(
    features, strips, senders, edge_basis, w_recv, w_basis, w_out, sums, filter_rows, w_mix, plan
):
    degree, cols, low, members, lines, share, norm_factor = plan
    atom_rows, channels = features.shape
    grid_rows = sums.shape[0]
    step = 64
    pool_rows = sum(strip.shape[0] for strip in strips)
    dma = pltpu.SemaphoreType.DMA
    return pl.pallas_call(
        lambda *refs: fused_kernel(plan, *refs),
        grid=(atom_rows // step,),
        in_specs=[
            pl.BlockSpec((step * degree,), lambda i: (i,), memory_space=pltpu.SMEM),
            *[whole(strip.shape) for strip in strips],
            pl.BlockSpec((edge_basis.shape[0], step * degree), lambda i: (0, i)),
            pl.BlockSpec((step, channels), lambda i: (i, 0)),
            whole(w_recv.shape),
            whole(w_basis.shape),
            whole(w_out.shape),
            whole(sums.shape),
            whole(filter_rows.shape),
            whole(w_mix.shape),
        ],
        out_specs=[
            pl.BlockSpec((step, channels), lambda i: (i, 0)),
            whole((2 * grid_rows, channels)),
        ],
        out_shape=[
            jax.ShapeDtypeStruct((atom_rows, channels), jnp.float32),
            jax.ShapeDtypeStruct((2 * grid_rows, channels), jnp.float32),
        ],
        scratch_shapes=[
            pltpu.VMEM((pool_rows, 8, channels), jnp.float32),
            pltpu.VMEM((step, channels), jnp.float32),
            pltpu.VMEM((step, channels), jnp.float32),
            pltpu.VMEM((members - 1, lines * share, 2 * channels), jnp.float32),
            pltpu.VMEM((lines * share, 2 * channels), jnp.float32),
            pltpu.VMEM((lines - 1, share, 2 * channels), jnp.float32),
            pltpu.VMEM((lines, 2 * share, channels), jnp.bfloat16),
            pltpu.VMEM((members, lines, 2 * share, channels), jnp.bfloat16),
            dma((members - 1,)),
            dma((members - 1,)),
            dma((lines - 1,)),
            dma((lines - 1,)),
            dma((lines - 1,)),
            dma((lines - 1,)),
            dma((members - 1,)),
            dma((members - 1,)),
        ],
        compiler_params=pltpu.CompilerParams(
            vmem_limit_bytes=56 * MIB, collective_id=0, has_side_effects=True
        ),
        cost_estimate=pl.CostEstimate(
            flops=atom_rows * degree * channels * 200,
            bytes_accessed=atom_rows * degree * channels * 16,
            transcendentals=atom_rows * degree * channels,
        ),
        name="edges",
    )(
        senders, *strips, edge_basis, features, w_recv, w_basis, w_out, sums, filter_rows, w_mix
    )


def shifted(cells, axis, by):
    count = lax.axis_size(axis)
    return lax.ppermute(cells, axis, [(i, (i + by) % count) for i in range(count)])


def per_device(
    features,
    positions,
    atom_count,
    kgrid,
    k_filter,
    w_mix,
    w_recv,
    w_send,
    w_basis,
    w_out,
    edge_basis,
    senders,
):
    atom_rows, channels = features.shape
    degree = senders.shape[0] // atom_rows
    total_k = kgrid.shape[1]
    devices = lax.axis_size(("slab", "sub"))
    cols = lax.axis_size("sub")
    unit = devices * 8
    grid_rows = -(-SIDE * PAIRS // unit) * unit
    share = grid_rows // devices
    norm_factor = 1.0 / math.sqrt(atom_rows * devices)
    live_mask = (jnp.arange(atom_rows, dtype=jnp.int32) < atom_count[0]).astype(jnp.float32)
    masked = (features.astype(jnp.float32) * live_mask[:, None]).astype(jnp.bfloat16)

    send_proj = jnp.dot(features, w_send, preferred_element_type=jnp.float32).astype(jnp.bfloat16)
    if cols == 2:
        strip = jnp.stack([send_proj, shifted(send_proj, "sub", 1)])
    else:
        strip = jnp.stack([shifted(send_proj, "sub", 1), send_proj, shifted(send_proj, "sub", -1)])
    strip = strip.reshape(-1, channels)
    strips = (shifted(strip, "slab", 1), strip, shifted(strip, "slab", -1))
    if cols == 2:
        block = senders // atom_rows
        slab_step = block // 3
        col_step = block - 3 * slab_step
        senders = (slab_step * 2 + (col_step != 1)) * atom_rows + (senders - block * atom_rows)

    steps = jnp.arange(16, dtype=jnp.float32)
    waves = jnp.concatenate([steps, steps - KMAX, steps - KMAX])
    turns = waves[:, None] * jnp.repeat(positions, 16, axis=0)
    angles = (turns - jnp.round(turns)) * (2.0 * math.pi)
    table, sums = pl.pallas_call(
        table_kernel,
        out_shape=[
            jax.ShapeDtypeStruct((2 * grid_rows, atom_rows), jnp.bfloat16),
            jax.ShapeDtypeStruct((grid_rows, 2 * channels), jnp.float32),
        ],
        scratch_shapes=[pltpu.VMEM((PAIRS, atom_rows), jnp.float32)] * 2,
        compiler_params=pltpu.CompilerParams(vmem_limit_bytes=32 * MIB),
        name="factors",
    )(jnp.cos(angles), jnp.sin(angles), masked)

    low = 4
    lines = lax.axis_size("slab") // low
    members = low * cols
    slab, sub = lax.axis_index("slab"), lax.axis_index("sub")
    piece = ((slab % low) * cols + sub) * lines + slab // low
    flip = jnp.where(kgrid[0] < 0, -1, 1)
    grid_of_k = (kgrid[2] * flip + KMAX) * PAIRS + kgrid[0] * flip * SIDE + kgrid[1] * flip + KMAX
    my_rows = piece * share + jnp.arange(share, dtype=jnp.int32)
    picks = (my_rows[:, None] == grid_of_k[None, :]).astype(jnp.float32)
    filter_sum = jnp.dot(
        picks, k_filter, precision=lax.Precision.HIGHEST, preferred_element_type=jnp.float32
    )
    filter_rows = jnp.concatenate([filter_sum, filter_sum])
    plan = (degree, cols, low, members, lines, share, norm_factor)
    aggregate, factors = edges_and_factors(
        features, strips, senders, edge_basis, w_recv, w_basis, w_out, sums, filter_rows, w_mix, plan
    )
    return pl.pallas_call(
        lambda *refs: finish_kernel(4.0 / math.sqrt(total_k), *refs),
        out_shape=jax.ShapeDtypeStruct((atom_rows, channels), jnp.float32),
        compiler_params=pltpu.CompilerParams(vmem_limit_bytes=32 * MIB),
        name="finish",
    )(table, factors, aggregate, live_mask[:, None])


def solution(mesh):
    placed = (
        P(("slab", "sub"), None),
        P(None, ("slab", "sub")),
        P(("slab", "sub")),
        P(),
        P(),
        P(),
        P(),
        P(),
        P(),
        P(),
        P(None, ("slab", "sub")),
        P(("slab", "sub")),
    )
    return jax.shard_map(
        per_device, mesh=mesh, in_specs=placed, out_specs=P(("slab", "sub"), None), check_vma=False
    )
```

```python
import math

import jax
import jax.numpy as jnp
from jax import lax
from jax.experimental import pallas as pl
from jax.experimental.pallas import tpu as pltpu
from jax.sharding import PartitionSpec as P

KMAX = 6
SIDE = 2 * KMAX + 1
PAIRS = 96
MIB = 1024 * 1024
CONTRACT_FIRST = (((0,), (0,)), ((), ()))


def fill_tables(base_cos, base_sin, masked_ref, table_ref, sums_ref, pair_cos, pair_sin):
    grid_rows = table_ref.shape[0] // 2
    channels = masked_ref.shape[1]
    atom_rows = masked_ref.shape[0]
    for a in range(KMAX + 1):
        cx, sx = base_cos[a : a + 1, :], base_sin[a : a + 1, :]
        cy, sy = base_cos[16 : 16 + SIDE, :], base_sin[16 : 16 + SIDE, :]
        pair_cos[a * SIDE : (a + 1) * SIDE, :] = cx * cy - sx * sy
        pair_sin[a * SIDE : (a + 1) * SIDE, :] = sx * cy + cx * sy
    used = (KMAX + 1) * SIDE
    pair_cos[used:, :] = jnp.zeros((PAIRS - used, atom_rows), jnp.float32)
    pair_sin[used:, :] = jnp.zeros((PAIRS - used, atom_rows), jnp.float32)

    def one_plane(q, carry):
        cz, sz = base_cos[pl.ds(32 + q, 1), :], base_sin[pl.ds(32 + q, 1), :]
        cosines = (pair_cos[...] * cz - pair_sin[...] * sz).astype(jnp.bfloat16)
        sines = (pair_sin[...] * cz + pair_cos[...] * sz).astype(jnp.bfloat16)
        at = pl.multiple_of(q * PAIRS, PAIRS)
        table_ref[pl.ds(at, PAIRS), :] = cosines
        table_ref[pl.ds(at + grid_rows, PAIRS), :] = sines
        sums_ref[pl.ds(at, PAIRS), :channels] = jnp.dot(
            cosines, masked_ref[...], preferred_element_type=jnp.float32
        ).astype(jnp.bfloat16).astype(jnp.bfloat16)
        sums_ref[pl.ds(at, PAIRS), channels:] = jnp.dot(
            sines, masked_ref[...], preferred_element_type=jnp.float32
        ).astype(jnp.bfloat16)
        return carry

    lax.fori_loop(0, SIDE, one_plane, 0)
    tail = grid_rows - SIDE * PAIRS
    if tail:
        for start in (SIDE * PAIRS, grid_rows + SIDE * PAIRS):
            table_ref[start : start + tail, :] = jnp.zeros((tail, atom_rows), jnp.bfloat16)
        sums_ref[SIDE * PAIRS :, :] = jnp.zeros((tail, 2 * channels), jnp.bfloat16)


def edge_rows(degree, group, it, snd_ref, pool, basis_ref, w_basis, recv, total):
    edges = group * degree
    first = pl.multiple_of(it * edges, edges)
    row = pl.multiple_of(it * group, group)
    sublane = lax.broadcasted_iota(jnp.int32, pool.shape[1:], 0)
    recv_rows = recv[pl.ds(row, group), :]
    together = 128 // degree
    sums = []
    for j in range(group):
        if j % together == 0:
            radial = lax.dot_general(
                basis_ref[:, pl.ds(pl.multiple_of(first + j * degree, 128), 128)],
                w_basis[...],
                CONTRACT_FIRST,
                preferred_element_type=jnp.float32,
            )
        octets = []
        for octet in range(degree // 8):
            start = first + j * degree + octet * 8
            picked = pool[snd_ref[start]]
            for k in range(1, 8):
                picked = jnp.where(sublane == k, pool[snd_ref[start + k]], picked)
            octets.append(picked)
        gathered = jnp.concatenate(octets, axis=0)
        at = j % together * degree
        v = gathered + radial[at : at + degree, :] + recv_rows[j : j + 1, :]
        half = 0.5 * v
        hidden = (half + half * jnp.tanh(half)).astype(jnp.bfloat16)
        sums.append(jnp.sum(hidden.astype(jnp.float32), axis=0, keepdims=True))
    total[pl.ds(row, group), :] = jnp.concatenate(sums, axis=0)


def fused_kernel(
    plan,
    snd_ref,
    basis_ref,
    feat_ref,
    count_ref,
    base_cos,
    base_sin,
    w_send,
    w_recv,
    w_basis,
    w_out,
    filter_ref,
    w_mix,
    out_ref,
    strips,
    pool,
    masked,
    pair_cos,
    pair_sin,
    table,
    sums_ref,
    factor_ref,
    recv,
    total,
    in_plane,
    part,
    in_line,
    line_rows,
    plane_rows,
    send_a,
    recv_a,
    send_b,
    recv_b,
    send_c,
    recv_c,
    send_d,
    recv_d,
    send_x,
    recv_x,
    send_z,
    recv_z,
):
    degree, cols, low, members, lines, share, norm_factor, scale = plan
    block_rows, channels = feat_ref.shape
    slabs = low * lines
    home = 0 if cols == 2 else 1
    blocks = strips.shape[1]
    step = pl.program_id(0)
    slab, sub = lax.axis_index("slab"), lax.axis_index("sub")
    line = slab // low
    member = (slab % low) * cols + sub
    chunk = lines * share

    def plane_peer(r):
        peer = (member + r) % members
        return peer, {"slab": line * low + peer // cols, "sub": peer % cols}

    def line_peer(r):
        peer = (line + r) % lines
        return peer, {"slab": peer * low + slab % low, "sub": sub}

    def copy_a(r):
        peer, where = plane_peer(r)
        rows = pl.ds(pl.multiple_of(peer * chunk, 16), chunk)
        return pltpu.make_async_remote_copy(
            src_ref=sums_ref.at[rows],
            dst_ref=in_plane.at[r - 1],
            send_sem=send_a.at[r - 1],
            recv_sem=recv_a.at[r - 1],
            device_id=where,
            device_id_type=pl.DeviceIdType.MESH,
        )

    def copy_b(r):
        peer, where = line_peer(r)
        rows = pl.ds(pl.multiple_of(peer * share, 8), share)
        return pltpu.make_async_remote_copy(
            src_ref=part.at[rows],
            dst_ref=in_line.at[r - 1],
            send_sem=send_b.at[r - 1],
            recv_sem=recv_b.at[r - 1],
            device_id=where,
            device_id_type=pl.DeviceIdType.MESH,
        )

    def copy_c(r):
        peer, where = line_peer(r)
        return pltpu.make_async_remote_copy(
            src_ref=line_rows.at[line],
            dst_ref=line_rows.at[line],
            send_sem=send_c.at[r - 1],
            recv_sem=recv_c.at[r - 1],
            device_id=where,
            device_id_type=pl.DeviceIdType.MESH,
        )

    def copy_d(r):
        peer, where = plane_peer(r)
        return pltpu.make_async_remote_copy(
            src_ref=line_rows,
            dst_ref=plane_rows.at[member],
            send_sem=send_d.at[r - 1],
            recv_sem=recv_d.at[r - 1],
            device_id=where,
            device_id_type=pl.DeviceIdType.MESH,
        )

    def each(count, action):
        def one(r, carry):
            action(r)
            return carry

        lax.fori_loop(1, count, one, 0)

    sides = [(1, 1)] if cols == 2 else [(1, 0), (-1, 2)]

    def column_of(by):
        return {"slab": slab, "sub": (sub + by + cols) % cols}

    def slab_of(by):
        return {"slab": (slab + by + slabs) % slabs, "sub": sub}

    def copy_x(n):
        by, slot = sides[n]
        return pltpu.make_async_remote_copy(
            src_ref=strips.at[1, home],
            dst_ref=strips.at[1, slot],
            send_sem=send_x.at[n],
            recv_sem=recv_x.at[n],
            device_id=column_of(by),
            device_id_type=pl.DeviceIdType.MESH,
        )

    def copy_z(up, c):
        return pltpu.make_async_remote_copy(
            src_ref=strips.at[1, c],
            dst_ref=strips.at[0 if up else 2, c],
            send_sem=send_z.at[up * blocks + c],
            recv_sem=recv_z.at[up * blocks + c],
            device_id=slab_of(1 if up else -1),
            device_id_type=pl.DeviceIdType.MESH,
        )

    def spread(a, c):
        base = (a * blocks + c) * block_rows

        def some(n, carry):
            at = pl.multiple_of(n * 16, 16)
            rows = strips[a, c, pl.ds(at, 16), :].astype(jnp.float32)
            pool[pl.ds(base + at, 16)] = jnp.broadcast_to(rows[:, None, :], (16, 8, channels))
            return carry

        lax.fori_loop(0, block_rows // 16, some, 0)

    def live(width):
        rows = lax.broadcasted_iota(jnp.int32, (block_rows, width), 0)
        return rows < count_ref[0]

    @pl.when(step == 0)
    def _():
        strips[1, home] = jnp.dot(
            feat_ref[...], w_send[...], preferred_element_type=jnp.float32
        ).astype(jnp.bfloat16)
        barrier = pltpu.get_barrier_semaphore()

        def greet(where):
            pl.semaphore_signal(
                barrier, inc=1, device_id=where, device_id_type=pl.DeviceIdType.MESH
            )

        each(members, lambda r: greet(plane_peer(r)[1]))
        each(lines, lambda r: greet(line_peer(r)[1]))
        for by, slot in sides:
            greet(column_of(by))
        greet(slab_of(1))
        greet(slab_of(-1))
        pl.semaphore_wait(barrier, members + lines + len(sides))
        for n in range(len(sides)):
            copy_x(n).start()
        for up in (1, 0):
            copy_z(up, home).start()
        masked[...] = jnp.where(live(channels), feat_ref[...].astype(jnp.float32), 0.0).astype(
            jnp.bfloat16
        )
        fill_tables(base_cos, base_sin, masked, table, sums_ref, pair_cos, pair_sin)
        for n, (by, slot) in enumerate(sides):
            copy_x(n).wait_recv()
            for up in (1, 0):
                copy_z(up, slot).start()
        each(members, lambda r: copy_a(r).start())
        recv[...] = jnp.dot(feat_ref[...], w_recv[...], preferred_element_type=jnp.float32)
        for c in range(blocks):
            spread(1, c)
        for c in [home] + [slot for by, slot in sides]:
            for up in (1, 0):
                copy_z(up, c).wait_recv()
                spread(0 if up else 2, c)

    @pl.when(step == 3)
    def _():
        each(members, lambda r: copy_a(r).wait_recv())
        part[...] = sums_ref[pl.ds(pl.multiple_of(member * chunk, 16), chunk), :].astype(jnp.float32)

        def add(r):
            part[...] += in_plane[r - 1].astype(jnp.float32)

        each(members, add)
        each(lines, lambda r: copy_b(r).start())

    @pl.when(step == 6)
    def _():
        each(lines, lambda r: copy_b(r).wait_recv())
        owned = part[pl.ds(pl.multiple_of(line * share, 8), share), :]
        for r in range(1, lines):
            owned = owned + in_line[r - 1]
        stacked = jnp.concatenate([owned[:, :channels], owned[:, channels:]], axis=0)
        scaled = stacked * norm_factor * filter_ref[...]
        line_rows[line] = jnp.dot(
            scaled,
            w_mix[...],
            precision=lax.Precision.HIGHEST,
            preferred_element_type=jnp.float32,
        ).astype(jnp.bfloat16)
        each(lines, lambda r: copy_c(r).start())

    @pl.when(step == 9)
    def _():
        each(lines, lambda r: copy_c(r).wait_recv())
        each(members, lambda r: copy_d(r).start())

    atoms = snd_ref.shape[0] // degree
    group = 16

    def some_atoms(it, carry):
        edge_rows(degree, group, it, snd_ref, pool, basis_ref, w_basis, recv_now, total_now)
        return carry

    here = pl.ds(pl.multiple_of(step * atoms, atoms), atoms)
    recv_now, total_now = recv.at[here], total.at[here]
    lax.fori_loop(0, atoms // group, some_atoms, 0)

    @pl.when(step == pl.num_programs(0) - 1)
    def _():
        for n in range(len(sides)):
            copy_x(n).wait_send()
        for up in (1, 0):
            for c in range(blocks):
                copy_z(up, c).wait_send()
        each(members, lambda r: copy_a(r).wait_send())
        each(lines, lambda r: copy_b(r).wait_send())
        each(lines, lambda r: copy_c(r).wait_send())
        each(members, lambda r: copy_d(r).wait())
        plane_rows[member] = line_rows[...]
        grid_rows = factor_ref.shape[0] // 2

        def lay(n, carry):
            rows = plane_rows[n // lines, n % lines].astype(jnp.float32)
            factor_ref[pl.ds(pl.multiple_of(n * share, 8), share), :] = rows[:share]
            factor_ref[pl.ds(pl.multiple_of(grid_rows + n * share, 8), share), :] = rows[share:]
            return carry

        lax.fori_loop(0, members * lines, lay, 0)
        spread_t = lax.dot_general(
            factor_ref[...].astype(jnp.bfloat16),
            table[...],
            CONTRACT_FIRST,
            preferred_element_type=jnp.float32,
        )
        high = total[...].astype(jnp.bfloat16)
        low_part = (total[...] - high.astype(jnp.float32)).astype(jnp.bfloat16)
        aggregate = (
            jnp.dot(high, w_out[...], preferred_element_type=jnp.float32)
            + jnp.dot(low_part, w_out[...], preferred_element_type=jnp.float32)
        ) * (1.0 / math.sqrt(degree))
        out_ref[...] = jnp.where(live(channels), aggregate + spread_t.T * scale, 0.0)


def whole(shape):
    return pl.BlockSpec(shape, lambda i: (0,) * len(shape), pipeline_mode=pl.Buffered(1))


def force_step(
    features, atom_count, senders, edge_basis, base_cos, base_sin, weights, filter_rows, w_mix, plan
):
    degree, cols, low, members, lines, share, norm_factor, scale = plan
    atom_rows, channels = features.shape
    grid_rows = members * lines * share
    blocks = 2 if cols == 2 else 3
    step = 64
    dma = pltpu.SemaphoreType.DMA
    f32, bf16 = jnp.float32, jnp.bfloat16
    return pl.pallas_call(
        lambda *refs: fused_kernel(plan, *refs),
        grid=(atom_rows // step,),
        in_specs=[
            pl.BlockSpec((step * degree,), lambda i: (i,), memory_space=pltpu.SMEM),
            pl.BlockSpec((edge_basis.shape[0], step * degree), lambda i: (0, i)),
            whole(features.shape),
            pl.BlockSpec(memory_space=pltpu.SMEM),
            whole(base_cos.shape),
            whole(base_sin.shape),
            *[whole(weight.shape) for weight in weights],
            whole(filter_rows.shape),
            whole(w_mix.shape),
        ],
        out_specs=whole((atom_rows, channels)),
        out_shape=jax.ShapeDtypeStruct((atom_rows, channels), f32),
        scratch_shapes=[
            pltpu.VMEM((3, blocks, atom_rows, channels), bf16),
            pltpu.VMEM((3 * blocks * atom_rows, 8, channels), f32),
            pltpu.VMEM((atom_rows, channels), bf16),
            pltpu.VMEM((PAIRS, atom_rows), f32),
            pltpu.VMEM((PAIRS, atom_rows), f32),
            pltpu.VMEM((2 * grid_rows, atom_rows), bf16),
            pltpu.VMEM((grid_rows, 2 * channels), bf16),
            pltpu.VMEM((2 * grid_rows, channels), f32),
            pltpu.VMEM((atom_rows, channels), f32),
            pltpu.VMEM((atom_rows, channels), f32),
            pltpu.VMEM((members - 1, lines * share, 2 * channels), bf16),
            pltpu.VMEM((lines * share, 2 * channels), f32),
            pltpu.VMEM((lines - 1, share, 2 * channels), f32),
            pltpu.VMEM((lines, 2 * share, channels), bf16),
            pltpu.VMEM((members, lines, 2 * share, channels), bf16),
            *[dma((members - 1,))] * 2,
            *[dma((lines - 1,))] * 4,
            *[dma((members - 1,))] * 2,
            *[dma((blocks - 1,))] * 2,
            *[dma((2 * blocks,))] * 2,
        ],
        compiler_params=pltpu.CompilerParams(
            vmem_limit_bytes=62 * MIB, collective_id=0, has_side_effects=True
        ),
        cost_estimate=pl.CostEstimate(
            flops=atom_rows * degree * channels * 200,
            bytes_accessed=atom_rows * degree * channels * 16,
            transcendentals=atom_rows * degree * channels,
        ),
        name="force_step",
    )(
        senders, edge_basis, features, atom_count, base_cos, base_sin, *weights, filter_rows, w_mix
    )


def per_device(
    features,
    positions,
    atom_count,
    kgrid,
    k_filter,
    w_mix,
    w_recv,
    w_send,
    w_basis,
    w_out,
    edge_basis,
    senders,
):
    atom_rows, channels = features.shape
    degree = senders.shape[0] // atom_rows
    total_k = kgrid.shape[1]
    devices = lax.axis_size(("slab", "sub"))
    cols = lax.axis_size("sub")
    unit = devices * 8
    grid_rows = -(-SIDE * PAIRS // unit) * unit
    share = grid_rows // devices
    norm_factor = 1.0 / math.sqrt(atom_rows * devices)
    if cols == 2:
        block = senders // atom_rows
        slab_step = block // 3
        col_step = block - 3 * slab_step
        senders = (slab_step * 2 + (col_step != 1)) * atom_rows + (senders - block * atom_rows)

    steps = jnp.arange(16, dtype=jnp.float32)
    waves = jnp.concatenate([steps, steps - KMAX, steps - KMAX])
    turns = waves[:, None] * jnp.repeat(positions, 16, axis=0)
    angles = (turns - jnp.round(turns)) * (2.0 * math.pi)
    low = 4
    lines = lax.axis_size("slab") // low
    members = low * cols
    slab, sub = lax.axis_index("slab"), lax.axis_index("sub")
    piece = ((slab % low) * cols + sub) * lines + slab // low
    flip = jnp.where(kgrid[0] < 0, -1, 1)
    grid_of_k = (kgrid[2] * flip + KMAX) * PAIRS + kgrid[0] * flip * SIDE + kgrid[1] * flip + KMAX
    my_rows = piece * share + jnp.arange(share, dtype=jnp.int32)
    picks = (my_rows[:, None] == grid_of_k[None, :]).astype(jnp.float32)
    filter_sum = jnp.dot(
        picks, k_filter, precision=lax.Precision.HIGHEST, preferred_element_type=jnp.float32
    )
    filter_rows = jnp.concatenate([filter_sum, filter_sum])
    plan = (degree, cols, low, members, lines, share, norm_factor, 4.0 / math.sqrt(total_k))
    weights = (w_send, w_recv, w_basis, w_out)
    return force_step(
        features,
        atom_count,
        senders,
        edge_basis,
        jnp.cos(angles),
        jnp.sin(angles),
        weights,
        filter_rows,
        w_mix,
        plan,
    )


def solution(mesh):
    placed = (
        P(("slab", "sub"), None),
        P(None, ("slab", "sub")),
        P(("slab", "sub")),
        P(),
        P(),
        P(),
        P(),
        P(),
        P(),
        P(),
        P(None, ("slab", "sub")),
        P(("slab", "sub")),
    )
    return jax.shard_map(
        per_device, mesh=mesh, in_specs=placed, out_specs=P(("slab", "sub"), None), check_vma=False
    )
```

```python
import math

import jax
import jax.numpy as jnp
from jax import lax
from jax.experimental import pallas as pl
from jax.experimental.pallas import tpu as pltpu
from jax.sharding import PartitionSpec as P

KMAX = 6
SIDE = 2 * KMAX + 1
PAIRS = 96
MIB = 1024 * 1024
CONTRACT_FIRST = (((0,), (0,)), ((), ()))


def fill_tables(base_cos, base_sin, masked_ref, table_ref, sums_ref, pair_cos, pair_sin):
    grid_rows = table_ref.shape[0] // 2
    channels = masked_ref.shape[1]
    atom_rows = masked_ref.shape[0]
    for a in range(KMAX + 1):
        cx, sx = base_cos[a : a + 1, :], base_sin[a : a + 1, :]
        cy, sy = base_cos[16 : 16 + SIDE, :], base_sin[16 : 16 + SIDE, :]
        pair_cos[a * SIDE : (a + 1) * SIDE, :] = cx * cy - sx * sy
        pair_sin[a * SIDE : (a + 1) * SIDE, :] = sx * cy + cx * sy
    used = (KMAX + 1) * SIDE
    pair_cos[used:, :] = jnp.zeros((PAIRS - used, atom_rows), jnp.float32)
    pair_sin[used:, :] = jnp.zeros((PAIRS - used, atom_rows), jnp.float32)

    def one_plane(q, carry):
        cz, sz = base_cos[pl.ds(32 + q, 1), :], base_sin[pl.ds(32 + q, 1), :]
        cosines = (pair_cos[...] * cz - pair_sin[...] * sz).astype(jnp.bfloat16)
        sines = (pair_sin[...] * cz + pair_cos[...] * sz).astype(jnp.bfloat16)
        at = pl.multiple_of(q * PAIRS, PAIRS)
        table_ref[pl.ds(at, PAIRS), :] = cosines
        table_ref[pl.ds(at + grid_rows, PAIRS), :] = sines
        sums_ref[pl.ds(at, PAIRS), :channels] = jnp.dot(
            cosines, masked_ref[...], preferred_element_type=jnp.float32
        ).astype(jnp.bfloat16).astype(jnp.bfloat16)
        sums_ref[pl.ds(at, PAIRS), channels:] = jnp.dot(
            sines, masked_ref[...], preferred_element_type=jnp.float32
        ).astype(jnp.bfloat16)
        return carry

    lax.fori_loop(0, SIDE, one_plane, 0)
    tail = grid_rows - SIDE * PAIRS
    if tail:
        for start in (SIDE * PAIRS, grid_rows + SIDE * PAIRS):
            table_ref[start : start + tail, :] = jnp.zeros((tail, atom_rows), jnp.bfloat16)
        sums_ref[SIDE * PAIRS :, :] = jnp.zeros((tail, 2 * channels), jnp.bfloat16)


def edge_rows(degree, group, it, snd_ref, pool, base, total):
    edges = group * degree
    first = pl.multiple_of(it * edges, edges)
    row = pl.multiple_of(it * group, group)
    sums = []
    for j in range(group):
        at = first + j * degree
        rows = [pool[pl.ds(snd_ref[at + e], 1), :] for e in range(degree)]
        half = jnp.concatenate(rows, axis=0) + base[pl.ds(pl.multiple_of(at, degree), degree), :]
        hidden = (half + half * jnp.tanh(half)).astype(jnp.bfloat16)
        sums.append(jnp.sum(hidden.astype(jnp.float32), axis=0, keepdims=True))
    total[pl.ds(row, group), :] = jnp.concatenate(sums, axis=0)


def edge_base(degree, basis_ref, w_basis, recv, base):
    atoms = 8
    edges = atoms * degree
    channels = recv.shape[1]

    def some(n, carry):
        first = pl.multiple_of(n * edges, edges)
        radial = lax.dot_general(
            basis_ref[:, pl.ds(first, edges)],
            w_basis[...],
            CONTRACT_FIRST,
            preferred_element_type=jnp.float32,
        )
        rows = recv[pl.ds(pl.multiple_of(n * atoms, atoms), atoms), :]
        both = radial.reshape(atoms, degree, channels) + rows[:, None, :]
        base[pl.ds(first, edges), :] = 0.5 * both.reshape(edges, channels)
        return carry

    lax.fori_loop(0, recv.shape[0] // atoms, some, 0)


def fused_kernel(
    plan,
    snd_ref,
    basis_ref,
    feat_ref,
    count_ref,
    base_cos,
    base_sin,
    w_send,
    w_recv,
    w_basis,
    w_out,
    filter_ref,
    w_mix,
    out_ref,
    strips,
    pool,
    masked,
    pair_cos,
    pair_sin,
    table,
    sums_ref,
    factor_ref,
    recv,
    base,
    total,
    in_plane,
    part,
    in_line,
    line_rows,
    plane_rows,
    send_a,
    recv_a,
    send_b,
    recv_b,
    send_c,
    recv_c,
    send_d,
    recv_d,
    send_x,
    recv_x,
    send_z,
    recv_z,
):
    degree, cols, low, members, lines, share, norm_factor, scale = plan
    block_rows, channels = feat_ref.shape
    slabs = low * lines
    home = 0 if cols == 2 else 1
    blocks = strips.shape[1]
    step = pl.program_id(0)
    slab, sub = lax.axis_index("slab"), lax.axis_index("sub")
    line = slab // low
    member = (slab % low) * cols + sub
    chunk = lines * share

    def plane_peer(r):
        peer = (member + r) % members
        return peer, {"slab": line * low + peer // cols, "sub": peer % cols}

    def line_peer(r):
        peer = (line + r) % lines
        return peer, {"slab": peer * low + slab % low, "sub": sub}

    def copy_a(r):
        peer, where = plane_peer(r)
        rows = pl.ds(pl.multiple_of(peer * chunk, 16), chunk)
        return pltpu.make_async_remote_copy(
            src_ref=sums_ref.at[rows],
            dst_ref=in_plane.at[r - 1],
            send_sem=send_a.at[r - 1],
            recv_sem=recv_a.at[r - 1],
            device_id=where,
            device_id_type=pl.DeviceIdType.MESH,
        )

    def copy_b(r):
        peer, where = line_peer(r)
        rows = pl.ds(pl.multiple_of(peer * share, 8), share)
        return pltpu.make_async_remote_copy(
            src_ref=part.at[rows],
            dst_ref=in_line.at[r - 1],
            send_sem=send_b.at[r - 1],
            recv_sem=recv_b.at[r - 1],
            device_id=where,
            device_id_type=pl.DeviceIdType.MESH,
        )

    def copy_c(r):
        peer, where = line_peer(r)
        return pltpu.make_async_remote_copy(
            src_ref=line_rows.at[line],
            dst_ref=line_rows.at[line],
            send_sem=send_c.at[r - 1],
            recv_sem=recv_c.at[r - 1],
            device_id=where,
            device_id_type=pl.DeviceIdType.MESH,
        )

    def copy_d(r):
        peer, where = plane_peer(r)
        return pltpu.make_async_remote_copy(
            src_ref=line_rows,
            dst_ref=plane_rows.at[member],
            send_sem=send_d.at[r - 1],
            recv_sem=recv_d.at[r - 1],
            device_id=where,
            device_id_type=pl.DeviceIdType.MESH,
        )

    def each(count, action):
        def one(r, carry):
            action(r)
            return carry

        lax.fori_loop(1, count, one, 0)

    sides = [(1, 1)] if cols == 2 else [(1, 0), (-1, 2)]

    def column_of(by):
        return {"slab": slab, "sub": (sub + by + cols) % cols}

    def slab_of(by):
        return {"slab": (slab + by + slabs) % slabs, "sub": sub}

    def copy_x(n):
        by, slot = sides[n]
        return pltpu.make_async_remote_copy(
            src_ref=strips.at[1, home],
            dst_ref=strips.at[1, slot],
            send_sem=send_x.at[n],
            recv_sem=recv_x.at[n],
            device_id=column_of(by),
            device_id_type=pl.DeviceIdType.MESH,
        )

    def copy_z(up, c):
        return pltpu.make_async_remote_copy(
            src_ref=strips.at[1, c],
            dst_ref=strips.at[0 if up else 2, c],
            send_sem=send_z.at[up * blocks + c],
            recv_sem=recv_z.at[up * blocks + c],
            device_id=slab_of(1 if up else -1),
            device_id_type=pl.DeviceIdType.MESH,
        )

    def spread(a, c):
        first = (a * blocks + c) * block_rows

        def some(n, carry):
            at = pl.multiple_of(n * 16, 16)
            rows = strips[a, c, pl.ds(at, 16), :].astype(jnp.float32)
            pool[pl.ds(pl.multiple_of(first + at, 16), 16), :] = 0.5 * rows
            return carry

        lax.fori_loop(0, block_rows // 16, some, 0)

    def live(width):
        rows = lax.broadcasted_iota(jnp.int32, (block_rows, width), 0)
        return rows < count_ref[0]

    @pl.when(step == 0)
    def _():
        strips[1, home] = jnp.dot(
            feat_ref[...], w_send[...], preferred_element_type=jnp.float32
        ).astype(jnp.bfloat16)
        barrier = pltpu.get_barrier_semaphore()

        def greet(where):
            pl.semaphore_signal(
                barrier, inc=1, device_id=where, device_id_type=pl.DeviceIdType.MESH
            )

        each(members, lambda r: greet(plane_peer(r)[1]))
        each(lines, lambda r: greet(line_peer(r)[1]))
        for by, slot in sides:
            greet(column_of(by))
        greet(slab_of(1))
        greet(slab_of(-1))
        pl.semaphore_wait(barrier, members + lines + len(sides))
        for n in range(len(sides)):
            copy_x(n).start()
        for up in (1, 0):
            copy_z(up, home).start()
        masked[...] = jnp.where(live(channels), feat_ref[...].astype(jnp.float32), 0.0).astype(
            jnp.bfloat16
        )
        fill_tables(base_cos, base_sin, masked, table, sums_ref, pair_cos, pair_sin)
        for n, (by, slot) in enumerate(sides):
            copy_x(n).wait_recv()
            for up in (1, 0):
                copy_z(up, slot).start()
        each(members, lambda r: copy_a(r).start())
        recv[...] = jnp.dot(feat_ref[...], w_recv[...], preferred_element_type=jnp.float32)
        edge_base(degree, basis_ref, w_basis, recv, base)
        for c in range(blocks):
            spread(1, c)
        for c in [home] + [slot for by, slot in sides]:
            for up in (1, 0):
                copy_z(up, c).wait_recv()
                spread(0 if up else 2, c)

    @pl.when(step == 3)
    def _():
        each(members, lambda r: copy_a(r).wait_recv())
        part[...] = sums_ref[pl.ds(pl.multiple_of(member * chunk, 16), chunk), :].astype(jnp.float32)

        def add(r):
            part[...] += in_plane[r - 1].astype(jnp.float32)

        each(members, add)
        each(lines, lambda r: copy_b(r).start())

    @pl.when(step == 6)
    def _():
        each(lines, lambda r: copy_b(r).wait_recv())
        owned = part[pl.ds(pl.multiple_of(line * share, 8), share), :]
        for r in range(1, lines):
            owned = owned + in_line[r - 1]
        stacked = jnp.concatenate([owned[:, :channels], owned[:, channels:]], axis=0)
        scaled = stacked * norm_factor * filter_ref[...]
        line_rows[line] = jnp.dot(
            scaled,
            w_mix[...],
            precision=lax.Precision.HIGHEST,
            preferred_element_type=jnp.float32,
        ).astype(jnp.bfloat16)
        each(lines, lambda r: copy_c(r).start())

    @pl.when(step == 9)
    def _():
        each(lines, lambda r: copy_c(r).wait_recv())
        each(members, lambda r: copy_d(r).start())

    atoms = snd_ref.shape[0] // degree
    group = 16

    def some_atoms(it, carry):
        edge_rows(degree, group, it, snd_ref, pool, base_now, total_now)
        return carry

    here = pl.ds(pl.multiple_of(step * atoms, atoms), atoms)
    total_now = total.at[here]
    base_now = base.at[pl.ds(pl.multiple_of(step * atoms * degree, atoms * degree), atoms * degree)]
    lax.fori_loop(0, atoms // group, some_atoms, 0)

    @pl.when(step == pl.num_programs(0) - 1)
    def _():
        for n in range(len(sides)):
            copy_x(n).wait_send()
        for up in (1, 0):
            for c in range(blocks):
                copy_z(up, c).wait_send()
        each(members, lambda r: copy_a(r).wait_send())
        each(lines, lambda r: copy_b(r).wait_send())
        each(lines, lambda r: copy_c(r).wait_send())
        each(members, lambda r: copy_d(r).wait())
        plane_rows[member] = line_rows[...]
        grid_rows = factor_ref.shape[0] // 2

        def lay(n, carry):
            rows = plane_rows[n // lines, n % lines].astype(jnp.float32)
            factor_ref[pl.ds(pl.multiple_of(n * share, 8), share), :] = rows[:share]
            factor_ref[pl.ds(pl.multiple_of(grid_rows + n * share, 8), share), :] = rows[share:]
            return carry

        lax.fori_loop(0, members * lines, lay, 0)
        spread_t = lax.dot_general(
            factor_ref[...].astype(jnp.bfloat16),
            table[...],
            CONTRACT_FIRST,
            preferred_element_type=jnp.float32,
        )
        high = total[...].astype(jnp.bfloat16)
        low_part = (total[...] - high.astype(jnp.float32)).astype(jnp.bfloat16)
        aggregate = (
            jnp.dot(high, w_out[...], preferred_element_type=jnp.float32)
            + jnp.dot(low_part, w_out[...], preferred_element_type=jnp.float32)
        ) * (1.0 / math.sqrt(degree))
        out_ref[...] = aggregate + spread_t.T * scale


def whole(shape):
    return pl.BlockSpec(shape, lambda i: (0,) * len(shape), pipeline_mode=pl.Buffered(1))


def force_step(
    features, atom_count, senders, edge_basis, base_cos, base_sin, weights, filter_rows, w_mix, plan
):
    degree, cols, low, members, lines, share, norm_factor, scale = plan
    atom_rows, channels = features.shape
    grid_rows = members * lines * share
    blocks = 2 if cols == 2 else 3
    step = 64
    dma = pltpu.SemaphoreType.DMA
    f32, bf16 = jnp.float32, jnp.bfloat16
    return pl.pallas_call(
        lambda *refs: fused_kernel(plan, *refs),
        grid=(atom_rows // step,),
        in_specs=[
            pl.BlockSpec((step * degree,), lambda i: (i,), memory_space=pltpu.SMEM),
            whole(edge_basis.shape),
            whole(features.shape),
            pl.BlockSpec(memory_space=pltpu.SMEM),
            whole(base_cos.shape),
            whole(base_sin.shape),
            *[whole(weight.shape) for weight in weights],
            whole(filter_rows.shape),
            whole(w_mix.shape),
        ],
        out_specs=whole((atom_rows, channels)),
        out_shape=jax.ShapeDtypeStruct((atom_rows, channels), f32),
        scratch_shapes=[
            pltpu.VMEM((3, blocks, atom_rows, channels), bf16),
            pltpu.VMEM((3 * blocks * atom_rows, channels), f32),
            pltpu.VMEM((atom_rows, channels), bf16),
            pltpu.VMEM((PAIRS, atom_rows), f32),
            pltpu.VMEM((PAIRS, atom_rows), f32),
            pltpu.VMEM((2 * grid_rows, atom_rows), bf16),
            pltpu.VMEM((grid_rows, 2 * channels), bf16),
            pltpu.VMEM((2 * grid_rows, channels), f32),
            pltpu.VMEM((atom_rows, channels), f32),
            pltpu.VMEM((atom_rows * degree, channels), f32),
            pltpu.VMEM((atom_rows, channels), f32),
            pltpu.VMEM((members - 1, lines * share, 2 * channels), bf16),
            pltpu.VMEM((lines * share, 2 * channels), f32),
            pltpu.VMEM((lines - 1, share, 2 * channels), f32),
            pltpu.VMEM((lines, 2 * share, channels), bf16),
            pltpu.VMEM((members, lines, 2 * share, channels), bf16),
            *[dma((members - 1,))] * 2,
            *[dma((lines - 1,))] * 4,
            *[dma((members - 1,))] * 2,
            *[dma((blocks - 1,))] * 2,
            *[dma((2 * blocks,))] * 2,
        ],
        compiler_params=pltpu.CompilerParams(
            vmem_limit_bytes=62 * MIB, collective_id=0, has_side_effects=True
        ),
        cost_estimate=pl.CostEstimate(
            flops=atom_rows * degree * channels * 200,
            bytes_accessed=atom_rows * degree * channels * 16,
            transcendentals=atom_rows * degree * channels,
        ),
        name="force_step",
    )(
        senders, edge_basis, features, atom_count, base_cos, base_sin, *weights, filter_rows, w_mix
    )


def per_device(
    features,
    positions,
    atom_count,
    kgrid,
    k_filter,
    w_mix,
    w_recv,
    w_send,
    w_basis,
    w_out,
    edge_basis,
    senders,
):
    atom_rows, channels = features.shape
    degree = senders.shape[0] // atom_rows
    total_k = kgrid.shape[1]
    devices = lax.axis_size(("slab", "sub"))
    cols = lax.axis_size("sub")
    unit = devices * 8
    grid_rows = -(-SIDE * PAIRS // unit) * unit
    share = grid_rows // devices
    norm_factor = 1.0 / math.sqrt(atom_rows * devices)
    if cols == 2:
        block = senders // atom_rows
        slab_step = block // 3
        col_step = block - 3 * slab_step
        senders = (slab_step * 2 + (col_step != 1)) * atom_rows + (senders - block * atom_rows)

    steps = jnp.arange(16, dtype=jnp.float32)
    waves = jnp.concatenate([steps, steps - KMAX, steps - KMAX])
    turns = waves[:, None] * jnp.repeat(positions, 16, axis=0)
    angles = (turns - jnp.round(turns)) * (2.0 * math.pi)
    low = 4
    lines = lax.axis_size("slab") // low
    members = low * cols
    slab, sub = lax.axis_index("slab"), lax.axis_index("sub")
    piece = ((slab % low) * cols + sub) * lines + slab // low
    flip = jnp.where(kgrid[0] < 0, -1, 1)
    grid_of_k = (kgrid[2] * flip + KMAX) * PAIRS + kgrid[0] * flip * SIDE + kgrid[1] * flip + KMAX
    my_rows = piece * share + jnp.arange(share, dtype=jnp.int32)
    picks = (my_rows[:, None] == grid_of_k[None, :]).astype(jnp.float32)
    filter_sum = jnp.dot(
        picks, k_filter, precision=lax.Precision.HIGHEST, preferred_element_type=jnp.float32
    )
    filter_rows = jnp.concatenate([filter_sum, filter_sum])
    plan = (degree, cols, low, members, lines, share, norm_factor, 4.0 / math.sqrt(total_k))
    weights = (w_send, w_recv, w_basis, w_out)
    unmasked = force_step(
        features,
        atom_count,
        senders,
        edge_basis,
        jnp.cos(angles),
        jnp.sin(angles),
        weights,
        filter_rows,
        w_mix,
        plan,
    )
    live = jnp.arange(atom_rows, dtype=jnp.int32) < atom_count[0]
    return jnp.where(live[:, None], unmasked, 0.0)


def solution(mesh):
    placed = (
        P(("slab", "sub"), None),
        P(None, ("slab", "sub")),
        P(("slab", "sub")),
        P(),
        P(),
        P(),
        P(),
        P(),
        P(),
        P(),
        P(None, ("slab", "sub")),
        P(("slab", "sub")),
    )
    return jax.shard_map(
        per_device, mesh=mesh, in_specs=placed, out_specs=P(("slab", "sub"), None), check_vma=False
    )
```

```python
import math

import jax
import jax.numpy as jnp
from jax import lax
from jax.experimental import pallas as pl
from jax.experimental.pallas import tpu as pltpu
from jax.sharding import PartitionSpec as P

KMAX = 6
SIDE = 2 * KMAX + 1
PAIRS = 96
MIB = 1024 * 1024
CONTRACT_FIRST = (((0,), (0,)), ((), ()))


def fill_tables(base_cos, base_sin, masked_ref, table_ref, sums_ref, pair_cos, pair_sin):
    grid_rows = table_ref.shape[0] // 2
    channels = masked_ref.shape[1]
    atom_rows = masked_ref.shape[0]
    for a in range(KMAX + 1):
        cx, sx = base_cos[a : a + 1, :], base_sin[a : a + 1, :]
        cy, sy = base_cos[16 : 16 + SIDE, :], base_sin[16 : 16 + SIDE, :]
        pair_cos[a * SIDE : (a + 1) * SIDE, :] = cx * cy - sx * sy
        pair_sin[a * SIDE : (a + 1) * SIDE, :] = sx * cy + cx * sy
    used = (KMAX + 1) * SIDE
    pair_cos[used:, :] = jnp.zeros((PAIRS - used, atom_rows), jnp.float32)
    pair_sin[used:, :] = jnp.zeros((PAIRS - used, atom_rows), jnp.float32)

    def one_plane(q, carry):
        cz, sz = base_cos[pl.ds(32 + q, 1), :], base_sin[pl.ds(32 + q, 1), :]
        cosines = (pair_cos[...] * cz - pair_sin[...] * sz).astype(jnp.bfloat16)
        sines = (pair_sin[...] * cz + pair_cos[...] * sz).astype(jnp.bfloat16)
        at = pl.multiple_of(q * PAIRS, PAIRS)
        table_ref[pl.ds(at, PAIRS), :] = cosines
        table_ref[pl.ds(at + grid_rows, PAIRS), :] = sines
        sums_ref[pl.ds(at, PAIRS), :channels] = jnp.dot(
            cosines, masked_ref[...], preferred_element_type=jnp.float32
        ).astype(jnp.bfloat16).astype(jnp.bfloat16)
        sums_ref[pl.ds(at, PAIRS), channels:] = jnp.dot(
            sines, masked_ref[...], preferred_element_type=jnp.float32
        ).astype(jnp.bfloat16)
        return carry

    lax.fori_loop(0, SIDE, one_plane, 0)
    tail = grid_rows - SIDE * PAIRS
    if tail:
        for start in (SIDE * PAIRS, grid_rows + SIDE * PAIRS):
            table_ref[start : start + tail, :] = jnp.zeros((tail, atom_rows), jnp.bfloat16)
        sums_ref[SIDE * PAIRS :, :] = jnp.zeros((tail, 2 * channels), jnp.bfloat16)


def edge_loop(degree, snd_ref, pool, base, base_first, total, total_first):
    group = 4
    edges = group * degree
    count = snd_ref.shape[0] // edges
    sublane = lax.broadcasted_iota(jnp.int32, pool.shape[1:], 0)
    masks = [sublane == k for k in range(8)]

    def gather(it):
        first = pl.multiple_of(it * edges, edges)
        parts = []
        for octet in range(edges // 8):
            start = first + octet * 8
            picked = pool[snd_ref[start]]
            for k in range(1, 8):
                picked = jnp.where(masks[k], pool[snd_ref[start + k]], picked)
            at = pl.multiple_of(base_first + first + octet * 8, 8)
            parts.append(picked + base[pl.ds(at, 8), :])
        return tuple(parts)

    def finish(it, halves):
        row = total_first + it * group
        for j in range(group):
            acc = None
            for half in halves[j * degree // 8 : (j + 1) * degree // 8]:
                hidden = (half + half * jnp.tanh(half)).astype(jnp.bfloat16).astype(jnp.float32)
                acc = hidden if acc is None else acc + hidden
            total[pl.ds(row + j, 1), :] = jnp.sum(acc, axis=0, keepdims=True)

    def one(it, halves):
        following = gather(it + 1)
        finish(it, halves)
        return following

    last = lax.fori_loop(0, count - 1, one, gather(0))
    finish(count - 1, last)


def edge_base(degree, basis_ref, w_basis, recv, base, start, count):
    atoms = 8
    edges = atoms * degree
    channels = recv.shape[1]

    def some(n, carry):
        first = pl.multiple_of(n * edges, edges)
        radial = lax.dot_general(
            basis_ref[:, pl.ds(pl.multiple_of(start * degree + first, edges), edges)],
            w_basis[...],
            CONTRACT_FIRST,
            preferred_element_type=jnp.float32,
        )
        rows = recv[pl.ds(pl.multiple_of(start + n * atoms, atoms), atoms), :]
        both = radial.reshape(atoms, degree, channels) + rows[:, None, :]
        base[pl.ds(first, edges), :] = 0.5 * both.reshape(edges, channels)
        return carry

    lax.fori_loop(0, count // atoms, some, 0)


def fused_kernel(
    plan,
    snd_ref,
    basis_ref,
    feat_ref,
    count_ref,
    base_cos,
    base_sin,
    w_send,
    w_recv,
    w_basis,
    w_out,
    filter_ref,
    w_mix,
    out_ref,
    strips,
    pool,
    masked,
    pair_cos,
    pair_sin,
    table,
    sums_ref,
    factor_ref,
    recv,
    base,
    total,
    in_plane,
    part,
    in_line,
    line_rows,
    plane_rows,
    send_a,
    recv_a,
    send_b,
    recv_b,
    send_c,
    recv_c,
    send_d,
    recv_d,
    send_x,
    recv_x,
    send_z,
    recv_z,
):
    degree, cols, low, members, lines, share, norm_factor, scale = plan
    block_rows, channels = feat_ref.shape
    slabs = low * lines
    home = 0 if cols == 2 else 1
    blocks = strips.shape[1]
    atoms = snd_ref.shape[0] // degree
    whole_base = base.shape[0] == block_rows * degree
    step = pl.program_id(0)
    slab, sub = lax.axis_index("slab"), lax.axis_index("sub")
    line = slab // low
    member = (slab % low) * cols + sub
    chunk = lines * share

    def plane_peer(r):
        peer = (member + r) % members
        return peer, {"slab": line * low + peer // cols, "sub": peer % cols}

    def line_peer(r):
        peer = (line + r) % lines
        return peer, {"slab": peer * low + slab % low, "sub": sub}

    def copy_a(r):
        peer, where = plane_peer(r)
        rows = pl.ds(pl.multiple_of(peer * chunk, 16), chunk)
        return pltpu.make_async_remote_copy(
            src_ref=sums_ref.at[rows],
            dst_ref=in_plane.at[r - 1],
            send_sem=send_a.at[r - 1],
            recv_sem=recv_a.at[r - 1],
            device_id=where,
            device_id_type=pl.DeviceIdType.MESH,
        )

    def copy_b(r):
        peer, where = line_peer(r)
        rows = pl.ds(pl.multiple_of(peer * share, 8), share)
        return pltpu.make_async_remote_copy(
            src_ref=part.at[rows],
            dst_ref=in_line.at[r - 1],
            send_sem=send_b.at[r - 1],
            recv_sem=recv_b.at[r - 1],
            device_id=where,
            device_id_type=pl.DeviceIdType.MESH,
        )

    def copy_c(r):
        peer, where = line_peer(r)
        return pltpu.make_async_remote_copy(
            src_ref=line_rows.at[line],
            dst_ref=line_rows.at[line],
            send_sem=send_c.at[r - 1],
            recv_sem=recv_c.at[r - 1],
            device_id=where,
            device_id_type=pl.DeviceIdType.MESH,
        )

    def copy_d(r):
        peer, where = plane_peer(r)
        return pltpu.make_async_remote_copy(
            src_ref=line_rows,
            dst_ref=plane_rows.at[member],
            send_sem=send_d.at[r - 1],
            recv_sem=recv_d.at[r - 1],
            device_id=where,
            device_id_type=pl.DeviceIdType.MESH,
        )

    def each(count, action):
        def one(r, carry):
            action(r)
            return carry

        lax.fori_loop(1, count, one, 0)

    sides = [(1, 1)] if cols == 2 else [(1, 0), (-1, 2)]

    def column_of(by):
        return {"slab": slab, "sub": (sub + by + cols) % cols}

    def slab_of(by):
        return {"slab": (slab + by + slabs) % slabs, "sub": sub}

    def copy_x(n):
        by, slot = sides[n]
        return pltpu.make_async_remote_copy(
            src_ref=strips.at[1, home],
            dst_ref=strips.at[1, slot],
            send_sem=send_x.at[n],
            recv_sem=recv_x.at[n],
            device_id=column_of(by),
            device_id_type=pl.DeviceIdType.MESH,
        )

    def copy_z(up, c):
        return pltpu.make_async_remote_copy(
            src_ref=strips.at[1, c],
            dst_ref=strips.at[0 if up else 2, c],
            send_sem=send_z.at[up * blocks + c],
            recv_sem=recv_z.at[up * blocks + c],
            device_id=slab_of(1 if up else -1),
            device_id_type=pl.DeviceIdType.MESH,
        )

    def spread(a, c):
        first = (a * blocks + c) * block_rows

        def some(n, carry):
            at = pl.multiple_of(n * 16, 16)
            rows = strips[a, c, pl.ds(at, 16), :].astype(jnp.float32)
            pool[pl.ds(first + at, 16)] = jnp.broadcast_to(
                (0.5 * rows)[:, None, :], (16, 8, channels)
            )
            return carry

        lax.fori_loop(0, block_rows // 16, some, 0)

    def live(width):
        rows = lax.broadcasted_iota(jnp.int32, (block_rows, width), 0)
        return rows < count_ref[0]

    @pl.when(step == 0)
    def _():
        strips[1, home] = jnp.dot(
            feat_ref[...], w_send[...], preferred_element_type=jnp.float32
        ).astype(jnp.bfloat16)
        barrier = pltpu.get_barrier_semaphore()

        def greet(where):
            pl.semaphore_signal(
                barrier, inc=1, device_id=where, device_id_type=pl.DeviceIdType.MESH
            )

        each(members, lambda r: greet(plane_peer(r)[1]))
        each(lines, lambda r: greet(line_peer(r)[1]))
        for by, slot in sides:
            greet(column_of(by))
        greet(slab_of(1))
        greet(slab_of(-1))
        pl.semaphore_wait(barrier, members + lines + len(sides))
        for n in range(len(sides)):
            copy_x(n).start()
        for up in (1, 0):
            copy_z(up, home).start()
        masked[...] = jnp.where(live(channels), feat_ref[...].astype(jnp.float32), 0.0).astype(
            jnp.bfloat16
        )
        fill_tables(base_cos, base_sin, masked, table, sums_ref, pair_cos, pair_sin)
        for n, (by, slot) in enumerate(sides):
            copy_x(n).wait_recv()
            for up in (1, 0):
                copy_z(up, slot).start()
        recv[...] = jnp.dot(feat_ref[...], w_recv[...], preferred_element_type=jnp.float32)
        if whole_base:
            edge_base(degree, basis_ref, w_basis, recv, base, 0, block_rows)
        for c in range(blocks):
            spread(1, c)
        for c in [home] + [slot for by, slot in sides]:
            for up in (1, 0):
                copy_z(up, c).wait_recv()
                if c == sides[-1][1] and up == 0:
                    each(members, lambda r: copy_a(r).start())
                spread(0 if up else 2, c)

    @pl.when(step == 2)
    def _():
        each(members, lambda r: copy_a(r).wait_recv())
        part[...] = sums_ref[pl.ds(pl.multiple_of(member * chunk, 16), chunk), :].astype(jnp.float32)

        def add(r):
            part[...] += in_plane[r - 1].astype(jnp.float32)

        each(members, add)
        each(lines, lambda r: copy_b(r).start())

    @pl.when(step == 4)
    def _():
        each(lines, lambda r: copy_b(r).wait_recv())
        owned = part[pl.ds(pl.multiple_of(line * share, 8), share), :]
        for r in range(1, lines):
            owned = owned + in_line[r - 1]
        stacked = jnp.concatenate([owned[:, :channels], owned[:, channels:]], axis=0)
        scaled = stacked * norm_factor * filter_ref[...]
        line_rows[line] = jnp.dot(
            scaled,
            w_mix[...],
            precision=lax.Precision.HIGHEST,
            preferred_element_type=jnp.float32,
        ).astype(jnp.bfloat16)
        each(lines, lambda r: copy_c(r).start())

    @pl.when(step == 5)
    def _():
        each(lines, lambda r: copy_c(r).wait_recv())
        each(members, lambda r: copy_d(r).start())

    row = pl.multiple_of(step * atoms, atoms)
    if not whole_base:
        edge_base(degree, basis_ref, w_basis, recv, base, row, atoms)
    edge_loop(degree, snd_ref, pool, base, row * degree if whole_base else 0, total, row)

    @pl.when(step == pl.num_programs(0) - 1)
    def _():
        for n in range(len(sides)):
            copy_x(n).wait_send()
        for up in (1, 0):
            for c in range(blocks):
                copy_z(up, c).wait_send()
        each(members, lambda r: copy_a(r).wait_send())
        each(lines, lambda r: copy_b(r).wait_send())
        each(lines, lambda r: copy_c(r).wait_send())
        each(members, lambda r: copy_d(r).wait())
        plane_rows[member] = line_rows[...]
        grid_rows = factor_ref.shape[0] // 2

        def lay(n, carry):
            rows = plane_rows[n // lines, n % lines].astype(jnp.float32)
            factor_ref[pl.ds(pl.multiple_of(n * share, 8), share), :] = rows[:share]
            factor_ref[pl.ds(pl.multiple_of(grid_rows + n * share, 8), share), :] = rows[share:]
            return carry

        lax.fori_loop(0, members * lines, lay, 0)
        spread_t = lax.dot_general(
            factor_ref[...].astype(jnp.bfloat16),
            table[...],
            CONTRACT_FIRST,
            preferred_element_type=jnp.float32,
        )
        high = total[...].astype(jnp.bfloat16)
        low_part = (total[...] - high.astype(jnp.float32)).astype(jnp.bfloat16)
        aggregate = (
            jnp.dot(high, w_out[...], preferred_element_type=jnp.float32)
            + jnp.dot(low_part, w_out[...], preferred_element_type=jnp.float32)
        ) * (1.0 / math.sqrt(degree))
        out_ref[...] = aggregate + spread_t.T * scale


def whole(shape):
    return pl.BlockSpec(shape, lambda i: (0,) * len(shape), pipeline_mode=pl.Buffered(1))


def force_step(
    features, atom_count, senders, edge_basis, base_cos, base_sin, weights, filter_rows, w_mix, plan
):
    degree, cols, low, members, lines, share, norm_factor, scale = plan
    atom_rows, channels = features.shape
    grid_rows = members * lines * share
    blocks = 2 if cols == 2 else 3
    step = 128
    base_atoms = atom_rows if cols == 2 else step
    dma = pltpu.SemaphoreType.DMA
    f32, bf16 = jnp.float32, jnp.bfloat16
    return pl.pallas_call(
        lambda *refs: fused_kernel(plan, *refs),
        grid=(atom_rows // step,),
        in_specs=[
            pl.BlockSpec((step * degree,), lambda i: (i,), memory_space=pltpu.SMEM),
            whole(edge_basis.shape),
            whole(features.shape),
            pl.BlockSpec(memory_space=pltpu.SMEM),
            whole(base_cos.shape),
            whole(base_sin.shape),
            *[whole(weight.shape) for weight in weights],
            whole(filter_rows.shape),
            whole(w_mix.shape),
        ],
        out_specs=whole((atom_rows, channels)),
        out_shape=jax.ShapeDtypeStruct((atom_rows, channels), f32),
        scratch_shapes=[
            pltpu.VMEM((3, blocks, atom_rows, channels), bf16),
            pltpu.VMEM((3 * blocks * atom_rows, 8, channels), f32),
            pltpu.VMEM((atom_rows, channels), bf16),
            pltpu.VMEM((PAIRS, atom_rows), f32),
            pltpu.VMEM((PAIRS, atom_rows), f32),
            pltpu.VMEM((2 * grid_rows, atom_rows), bf16),
            pltpu.VMEM((grid_rows, 2 * channels), bf16),
            pltpu.VMEM((2 * grid_rows, channels), f32),
            pltpu.VMEM((atom_rows, channels), f32),
            pltpu.VMEM((base_atoms * degree, channels), f32),
            pltpu.VMEM((atom_rows, channels), f32),
            pltpu.VMEM((members - 1, lines * share, 2 * channels), bf16),
            pltpu.VMEM((lines * share, 2 * channels), f32),
            pltpu.VMEM((lines - 1, share, 2 * channels), f32),
            pltpu.VMEM((lines, 2 * share, channels), bf16),
            pltpu.VMEM((members, lines, 2 * share, channels), bf16),
            *[dma((members - 1,))] * 2,
            *[dma((lines - 1,))] * 4,
            *[dma((members - 1,))] * 2,
            *[dma((blocks - 1,))] * 2,
            *[dma((2 * blocks,))] * 2,
        ],
        compiler_params=pltpu.CompilerParams(
            vmem_limit_bytes=62 * MIB, collective_id=0, has_side_effects=True
        ),
        cost_estimate=pl.CostEstimate(
            flops=atom_rows * degree * channels * 200,
            bytes_accessed=atom_rows * degree * channels * 16,
            transcendentals=atom_rows * degree * channels,
        ),
        name="force_step",
    )(
        senders, edge_basis, features, atom_count, base_cos, base_sin, *weights, filter_rows, w_mix
    )


def per_device(
    features,
    positions,
    atom_count,
    kgrid,
    k_filter,
    w_mix,
    w_recv,
    w_send,
    w_basis,
    w_out,
    edge_basis,
    senders,
):
    atom_rows, channels = features.shape
    degree = senders.shape[0] // atom_rows
    total_k = kgrid.shape[1]
    devices = lax.axis_size(("slab", "sub"))
    cols = lax.axis_size("sub")
    unit = devices * 8
    grid_rows = -(-SIDE * PAIRS // unit) * unit
    share = grid_rows // devices
    norm_factor = 1.0 / math.sqrt(atom_rows * devices)
    if cols == 2:
        block = senders // atom_rows
        slab_step = block // 3
        col_step = block - 3 * slab_step
        senders = (slab_step * 2 + (col_step != 1)) * atom_rows + (senders - block * atom_rows)

    steps = jnp.arange(16, dtype=jnp.float32)
    waves = jnp.concatenate([steps, steps - KMAX, steps - KMAX])
    turns = waves[:, None] * jnp.repeat(positions, 16, axis=0)
    angles = (turns - jnp.round(turns)) * (2.0 * math.pi)
    low = 4
    lines = lax.axis_size("slab") // low
    members = low * cols
    slab, sub = lax.axis_index("slab"), lax.axis_index("sub")
    piece = ((slab % low) * cols + sub) * lines + slab // low
    flip = jnp.where(kgrid[0] < 0, -1, 1)
    grid_of_k = (kgrid[2] * flip + KMAX) * PAIRS + kgrid[0] * flip * SIDE + kgrid[1] * flip + KMAX
    my_rows = piece * share + jnp.arange(share, dtype=jnp.int32)
    picks = (my_rows[:, None] == grid_of_k[None, :]).astype(jnp.float32)
    filter_sum = jnp.dot(
        picks, k_filter, precision=lax.Precision.HIGHEST, preferred_element_type=jnp.float32
    )
    filter_rows = jnp.concatenate([filter_sum, filter_sum])
    plan = (degree, cols, low, members, lines, share, norm_factor, 4.0 / math.sqrt(total_k))
    weights = (w_send, w_recv, w_basis, w_out)
    unmasked = force_step(
        features,
        atom_count,
        senders,
        edge_basis,
        jnp.cos(angles),
        jnp.sin(angles),
        weights,
        filter_rows,
        w_mix,
        plan,
    )
    live = jnp.arange(atom_rows, dtype=jnp.int32) < atom_count[0]
    return jnp.where(live[:, None], unmasked, 0.0)


def solution(mesh):
    placed = (
        P(("slab", "sub"), None),
        P(None, ("slab", "sub")),
        P(("slab", "sub")),
        P(),
        P(),
        P(),
        P(),
        P(),
        P(),
        P(),
        P(None, ("slab", "sub")),
        P(("slab", "sub")),
    )
    return jax.shard_map(
        per_device, mesh=mesh, in_specs=placed, out_specs=P(("slab", "sub"), None), check_vma=False
    )
```

```python
import math

import jax
import jax.numpy as jnp
from jax import lax
from jax.experimental import pallas as pl
from jax.experimental.pallas import tpu as pltpu
from jax.sharding import PartitionSpec as P

KMAX = 6
SIDE = 2 * KMAX + 1
PAIRS = 96
MIB = 1024 * 1024
CONTRACT_FIRST = (((0,), (0,)), ((), ()))


def fill_tables(base_cos, base_sin, masked_ref, table_ref, sums_ref, pair_cos, pair_sin):
    grid_rows = table_ref.shape[0] // 2
    channels = masked_ref.shape[1]
    atom_rows = masked_ref.shape[0]
    for a in range(KMAX + 1):
        cx, sx = base_cos[a : a + 1, :], base_sin[a : a + 1, :]
        cy, sy = base_cos[16 : 16 + SIDE, :], base_sin[16 : 16 + SIDE, :]
        pair_cos[a * SIDE : (a + 1) * SIDE, :] = cx * cy - sx * sy
        pair_sin[a * SIDE : (a + 1) * SIDE, :] = sx * cy + cx * sy
    used = (KMAX + 1) * SIDE
    pair_cos[used:, :] = jnp.zeros((PAIRS - used, atom_rows), jnp.float32)
    pair_sin[used:, :] = jnp.zeros((PAIRS - used, atom_rows), jnp.float32)

    def one_plane(q, carry):
        cz, sz = base_cos[pl.ds(32 + q, 1), :], base_sin[pl.ds(32 + q, 1), :]
        cosines = (pair_cos[...] * cz - pair_sin[...] * sz).astype(jnp.bfloat16)
        sines = (pair_sin[...] * cz + pair_cos[...] * sz).astype(jnp.bfloat16)
        at = pl.multiple_of(q * PAIRS, PAIRS)
        table_ref[pl.ds(at, PAIRS), :] = cosines
        table_ref[pl.ds(at + grid_rows, PAIRS), :] = sines
        sums_ref[pl.ds(at, PAIRS), :channels] = jnp.dot(
            cosines, masked_ref[...], preferred_element_type=jnp.float32
        ).astype(jnp.bfloat16).astype(jnp.bfloat16)
        sums_ref[pl.ds(at, PAIRS), channels:] = jnp.dot(
            sines, masked_ref[...], preferred_element_type=jnp.float32
        ).astype(jnp.bfloat16)
        return carry

    lax.fori_loop(0, SIDE, one_plane, 0)
    tail = grid_rows - SIDE * PAIRS
    if tail:
        for start in (SIDE * PAIRS, grid_rows + SIDE * PAIRS):
            table_ref[start : start + tail, :] = jnp.zeros((tail, atom_rows), jnp.bfloat16)
        sums_ref[SIDE * PAIRS :, :] = jnp.zeros((tail, 2 * channels), jnp.bfloat16)


def edge_loop(degree, snd_ref, pool, base, base_first, total, total_first):
    group = 4
    edges = group * degree
    count = snd_ref.shape[0] // edges
    sublane = lax.broadcasted_iota(jnp.int32, (8, pool.shape[1]), 0)
    masks = [sublane == k for k in range(8)]

    def gather(it):
        first = pl.multiple_of(it * edges, edges)
        parts = []
        for octet in range(edges // 8):
            start = first + octet * 8
            picked = pool[pl.ds(snd_ref[start], 8), :]
            for k in range(1, 8):
                picked = jnp.where(masks[k], pool[pl.ds(snd_ref[start + k], 8), :], picked)
            at = pl.multiple_of(base_first + first + octet * 8, 8)
            parts.append(picked + base[pl.ds(at, 8), :])
        return tuple(parts)

    def finish(it, halves):
        row = total_first + it * group
        for j in range(group):
            acc = None
            for half in halves[j * degree // 8 : (j + 1) * degree // 8]:
                hidden = (half + half * jnp.tanh(half)).astype(jnp.bfloat16).astype(jnp.float32)
                acc = hidden if acc is None else acc + hidden
            total[pl.ds(row + j, 1), :] = jnp.sum(acc, axis=0, keepdims=True)

    def one(it, halves):
        following = gather(it + 1)
        finish(it, halves)
        return following

    last = lax.fori_loop(0, count - 1, one, gather(0))
    finish(count - 1, last)


def edge_base(degree, basis_ref, w_basis, recv, base, start, count):
    atoms = 64
    edges = atoms * degree
    channels = recv.shape[1]

    def some(n, carry):
        first = pl.multiple_of(n * edges, edges)
        radial = lax.dot_general(
            basis_ref[:, pl.ds(pl.multiple_of(start * degree + first, edges), edges)],
            w_basis[...],
            CONTRACT_FIRST,
            preferred_element_type=jnp.float32,
        )
        rows = recv[pl.ds(pl.multiple_of(start + n * atoms, atoms), atoms), :]
        both = radial.reshape(atoms, degree, channels) + rows[:, None, :]
        base[pl.ds(first, edges), :] = 0.5 * both.reshape(edges, channels)
        return carry

    lax.fori_loop(0, count // atoms, some, 0)


def fused_kernel(
    plan,
    snd_ref,
    basis_ref,
    feat_ref,
    count_ref,
    base_cos,
    base_sin,
    w_send,
    w_recv,
    w_basis,
    w_out,
    filter_ref,
    w_mix,
    out_ref,
    strips,
    pool,
    masked,
    pair_cos,
    pair_sin,
    table,
    sums_ref,
    factor_ref,
    recv,
    base,
    total,
    in_plane,
    part,
    in_line,
    line_rows,
    plane_rows,
    send_a,
    recv_a,
    send_b,
    recv_b,
    send_c,
    recv_c,
    send_d,
    recv_d,
    send_x,
    recv_x,
    send_z,
    recv_z,
):
    degree, cols, low, members, lines, share, norm_factor, scale = plan
    block_rows, channels = feat_ref.shape
    slabs = low * lines
    home = 0 if cols == 2 else 1
    blocks = strips.shape[1]
    atoms = snd_ref.shape[0] // degree
    whole_base = base.shape[0] == block_rows * degree
    step = pl.program_id(0)
    slab, sub = lax.axis_index("slab"), lax.axis_index("sub")
    line = slab // low
    member = (slab % low) * cols + sub
    chunk = lines * share

    def plane_peer(r):
        peer = (member + r) % members
        return peer, {"slab": line * low + peer // cols, "sub": peer % cols}

    def line_peer(r):
        peer = (line + r) % lines
        return peer, {"slab": peer * low + slab % low, "sub": sub}

    def copy_a(r):
        peer, where = plane_peer(r)
        rows = pl.ds(pl.multiple_of(peer * chunk, 16), chunk)
        return pltpu.make_async_remote_copy(
            src_ref=sums_ref.at[rows],
            dst_ref=in_plane.at[r - 1],
            send_sem=send_a.at[r - 1],
            recv_sem=recv_a.at[r - 1],
            device_id=where,
            device_id_type=pl.DeviceIdType.MESH,
        )

    def copy_b(r):
        peer, where = line_peer(r)
        rows = pl.ds(pl.multiple_of(peer * share, 8), share)
        return pltpu.make_async_remote_copy(
            src_ref=part.at[rows],
            dst_ref=in_line.at[r - 1],
            send_sem=send_b.at[r - 1],
            recv_sem=recv_b.at[r - 1],
            device_id=where,
            device_id_type=pl.DeviceIdType.MESH,
        )

    def copy_c(r):
        peer, where = line_peer(r)
        return pltpu.make_async_remote_copy(
            src_ref=line_rows.at[line],
            dst_ref=line_rows.at[line],
            send_sem=send_c.at[r - 1],
            recv_sem=recv_c.at[r - 1],
            device_id=where,
            device_id_type=pl.DeviceIdType.MESH,
        )

    def copy_d(r):
        peer, where = plane_peer(r)
        return pltpu.make_async_remote_copy(
            src_ref=line_rows,
            dst_ref=plane_rows.at[member],
            send_sem=send_d.at[r - 1],
            recv_sem=recv_d.at[r - 1],
            device_id=where,
            device_id_type=pl.DeviceIdType.MESH,
        )

    def each(count, action):
        def one(r, carry):
            action(r)
            return carry

        lax.fori_loop(1, count, one, 0)

    sides = [(1, 1)] if cols == 2 else [(1, 0), (-1, 2)]

    def column_of(by):
        return {"slab": slab, "sub": (sub + by + cols) % cols}

    def slab_of(by):
        return {"slab": (slab + by + slabs) % slabs, "sub": sub}

    def copy_x(n):
        by, slot = sides[n]
        return pltpu.make_async_remote_copy(
            src_ref=strips.at[1, home],
            dst_ref=strips.at[1, slot],
            send_sem=send_x.at[n],
            recv_sem=recv_x.at[n],
            device_id=column_of(by),
            device_id_type=pl.DeviceIdType.MESH,
        )

    def copy_z(up, c):
        return pltpu.make_async_remote_copy(
            src_ref=strips.at[1, c],
            dst_ref=strips.at[0 if up else 2, c],
            send_sem=send_z.at[up * blocks + c],
            recv_sem=recv_z.at[up * blocks + c],
            device_id=slab_of(1 if up else -1),
            device_id_type=pl.DeviceIdType.MESH,
        )

    def spread(a, c):
        first = (a * blocks + c) * block_rows

        def some(n, carry):
            at = pl.multiple_of(n * 16, 16)
            rows = strips[a, c, pl.ds(at, 16), :].astype(jnp.float32)
            pool[pl.ds(pl.multiple_of(first + at + 8, 8), 16), :] = 0.5 * rows
            return carry

        lax.fori_loop(0, block_rows // 16, some, 0)

    def live(width):
        rows = lax.broadcasted_iota(jnp.int32, (block_rows, width), 0)
        return rows < count_ref[0]

    @pl.when(step == 0)
    def _():
        margin = jnp.zeros((8, channels), jnp.float32)
        pool[:8, :] = margin
        pool[pool.shape[0] - 8 :, :] = margin
        strips[1, home] = jnp.dot(
            feat_ref[...], w_send[...], preferred_element_type=jnp.float32
        ).astype(jnp.bfloat16)
        barrier = pltpu.get_barrier_semaphore()

        def greet(where):
            pl.semaphore_signal(
                barrier, inc=1, device_id=where, device_id_type=pl.DeviceIdType.MESH
            )

        each(members, lambda r: greet(plane_peer(r)[1]))
        each(lines, lambda r: greet(line_peer(r)[1]))
        for by, slot in sides:
            greet(column_of(by))
        greet(slab_of(1))
        greet(slab_of(-1))
        pl.semaphore_wait(barrier, members + lines + len(sides))
        for n in range(len(sides)):
            copy_x(n).start()
        for up in (1, 0):
            copy_z(up, home).start()
        masked[...] = jnp.where(live(channels), feat_ref[...].astype(jnp.float32), 0.0).astype(
            jnp.bfloat16
        )
        fill_tables(base_cos, base_sin, masked, table, sums_ref, pair_cos, pair_sin)
        for n, (by, slot) in enumerate(sides):
            copy_x(n).wait_recv()
            for up in (1, 0):
                copy_z(up, slot).start()
        recv[...] = jnp.dot(feat_ref[...], w_recv[...], preferred_element_type=jnp.float32)
        if whole_base:
            edge_base(degree, basis_ref, w_basis, recv, base, 0, block_rows)
        for c in range(blocks):
            spread(1, c)
        for c in [home] + [slot for by, slot in sides]:
            for up in (1, 0):
                copy_z(up, c).wait_recv()
                if c == sides[-1][1] and up == 0:
                    each(members, lambda r: copy_a(r).start())
                spread(0 if up else 2, c)

    @pl.when(step == 2)
    def _():
        each(members, lambda r: copy_a(r).wait_recv())
        part[...] = sums_ref[pl.ds(pl.multiple_of(member * chunk, 16), chunk), :].astype(jnp.float32)

        def add(r):
            part[...] += in_plane[r - 1].astype(jnp.float32)

        each(members, add)
        each(lines, lambda r: copy_b(r).start())

    @pl.when(step == 4)
    def _():
        each(lines, lambda r: copy_b(r).wait_recv())
        owned = part[pl.ds(pl.multiple_of(line * share, 8), share), :]
        for r in range(1, lines):
            owned = owned + in_line[r - 1]
        stacked = jnp.concatenate([owned[:, :channels], owned[:, channels:]], axis=0)
        scaled = stacked * norm_factor * filter_ref[...]
        line_rows[line] = jnp.dot(
            scaled,
            w_mix[...],
            precision=lax.Precision.HIGHEST,
            preferred_element_type=jnp.float32,
        ).astype(jnp.bfloat16)
        each(lines, lambda r: copy_c(r).start())

    @pl.when(step == 5)
    def _():
        each(lines, lambda r: copy_c(r).wait_recv())
        each(members, lambda r: copy_d(r).start())

    row = pl.multiple_of(step * atoms, atoms)
    if not whole_base:
        edge_base(degree, basis_ref, w_basis, recv, base, row, atoms)
    edge_loop(degree, snd_ref, pool, base, row * degree if whole_base else 0, total, row)

    @pl.when(step == pl.num_programs(0) - 1)
    def _():
        for n in range(len(sides)):
            copy_x(n).wait_send()
        for up in (1, 0):
            for c in range(blocks):
                copy_z(up, c).wait_send()
        each(members, lambda r: copy_a(r).wait_send())
        each(lines, lambda r: copy_b(r).wait_send())
        each(lines, lambda r: copy_c(r).wait_send())
        each(members, lambda r: copy_d(r).wait())
        plane_rows[member] = line_rows[...]
        grid_rows = factor_ref.shape[0] // 2

        def lay(n, carry):
            rows = plane_rows[n // lines, n % lines].astype(jnp.float32)
            factor_ref[pl.ds(pl.multiple_of(n * share, 8), share), :] = rows[:share]
            factor_ref[pl.ds(pl.multiple_of(grid_rows + n * share, 8), share), :] = rows[share:]
            return carry

        lax.fori_loop(0, members * lines, lay, 0)
        spread_t = lax.dot_general(
            factor_ref[...].astype(jnp.bfloat16),
            table[...],
            CONTRACT_FIRST,
            preferred_element_type=jnp.float32,
        )
        high = total[...].astype(jnp.bfloat16)
        low_part = (total[...] - high.astype(jnp.float32)).astype(jnp.bfloat16)
        aggregate = (
            jnp.dot(high, w_out[...], preferred_element_type=jnp.float32)
            + jnp.dot(low_part, w_out[...], preferred_element_type=jnp.float32)
        ) * (1.0 / math.sqrt(degree))
        out_ref[...] = aggregate + spread_t.T * scale


def whole(shape):
    return pl.BlockSpec(shape, lambda i: (0,) * len(shape), pipeline_mode=pl.Buffered(1))


def force_step(
    features, atom_count, senders, edge_basis, base_cos, base_sin, weights, filter_rows, w_mix, plan
):
    degree, cols, low, members, lines, share, norm_factor, scale = plan
    atom_rows, channels = features.shape
    grid_rows = members * lines * share
    blocks = 2 if cols == 2 else 3
    step = 128
    base_atoms = atom_rows
    dma = pltpu.SemaphoreType.DMA
    f32, bf16 = jnp.float32, jnp.bfloat16
    return pl.pallas_call(
        lambda *refs: fused_kernel(plan, *refs),
        grid=(atom_rows // step,),
        in_specs=[
            pl.BlockSpec((step * degree,), lambda i: (i,), memory_space=pltpu.SMEM),
            whole(edge_basis.shape),
            whole(features.shape),
            pl.BlockSpec(memory_space=pltpu.SMEM),
            whole(base_cos.shape),
            whole(base_sin.shape),
            *[whole(weight.shape) for weight in weights],
            whole(filter_rows.shape),
            whole(w_mix.shape),
        ],
        out_specs=whole((atom_rows, channels)),
        out_shape=jax.ShapeDtypeStruct((atom_rows, channels), f32),
        scratch_shapes=[
            pltpu.VMEM((3, blocks, atom_rows, channels), bf16),
            pltpu.VMEM((3 * blocks * atom_rows + 16, channels), f32),
            pltpu.VMEM((atom_rows, channels), bf16),
            pltpu.VMEM((PAIRS, atom_rows), f32),
            pltpu.VMEM((PAIRS, atom_rows), f32),
            pltpu.VMEM((2 * grid_rows, atom_rows), bf16),
            pltpu.VMEM((grid_rows, 2 * channels), bf16),
            pltpu.VMEM((2 * grid_rows, channels), f32),
            pltpu.VMEM((atom_rows, channels), f32),
            pltpu.VMEM((base_atoms * degree, channels), f32),
            pltpu.VMEM((atom_rows, channels), f32),
            pltpu.VMEM((members - 1, lines * share, 2 * channels), bf16),
            pltpu.VMEM((lines * share, 2 * channels), f32),
            pltpu.VMEM((lines - 1, share, 2 * channels), f32),
            pltpu.VMEM((lines, 2 * share, channels), bf16),
            pltpu.VMEM((members, lines, 2 * share, channels), bf16),
            *[dma((members - 1,))] * 2,
            *[dma((lines - 1,))] * 4,
            *[dma((members - 1,))] * 2,
            *[dma((blocks - 1,))] * 2,
            *[dma((2 * blocks,))] * 2,
        ],
        compiler_params=pltpu.CompilerParams(
            vmem_limit_bytes=62 * MIB, collective_id=0, has_side_effects=True
        ),
        cost_estimate=pl.CostEstimate(
            flops=atom_rows * degree * channels * 200,
            bytes_accessed=atom_rows * degree * channels * 16,
            transcendentals=atom_rows * degree * channels,
        ),
        name="force_step",
    )(
        senders, edge_basis, features, atom_count, base_cos, base_sin, *weights, filter_rows, w_mix
    )


def per_device(
    features,
    positions,
    atom_count,
    kgrid,
    k_filter,
    w_mix,
    w_recv,
    w_send,
    w_basis,
    w_out,
    edge_basis,
    senders,
):
    atom_rows, channels = features.shape
    degree = senders.shape[0] // atom_rows
    total_k = kgrid.shape[1]
    devices = lax.axis_size(("slab", "sub"))
    cols = lax.axis_size("sub")
    unit = devices * 8
    grid_rows = -(-SIDE * PAIRS // unit) * unit
    share = grid_rows // devices
    norm_factor = 1.0 / math.sqrt(atom_rows * devices)
    if cols == 2:
        block = senders // atom_rows
        slab_step = block // 3
        col_step = block - 3 * slab_step
        senders = (slab_step * 2 + (col_step != 1)) * atom_rows + (senders - block * atom_rows)

    senders = senders + (8 - jnp.arange(senders.shape[0], dtype=jnp.int32) % 8)

    steps = jnp.arange(16, dtype=jnp.float32)
    waves = jnp.concatenate([steps, steps - KMAX, steps - KMAX])
    turns = waves[:, None] * jnp.repeat(positions, 16, axis=0)
    angles = (turns - jnp.round(turns)) * (2.0 * math.pi)
    low = 4
    lines = lax.axis_size("slab") // low
    members = low * cols
    slab, sub = lax.axis_index("slab"), lax.axis_index("sub")
    piece = ((slab % low) * cols + sub) * lines + slab // low
    flip = jnp.where(kgrid[0] < 0, -1, 1)
    grid_of_k = (kgrid[2] * flip + KMAX) * PAIRS + kgrid[0] * flip * SIDE + kgrid[1] * flip + KMAX
    my_rows = piece * share + jnp.arange(share, dtype=jnp.int32)
    picks = (my_rows[:, None] == grid_of_k[None, :]).astype(jnp.float32)
    filter_sum = jnp.dot(
        picks, k_filter, precision=lax.Precision.HIGHEST, preferred_element_type=jnp.float32
    )
    filter_rows = jnp.concatenate([filter_sum, filter_sum])
    plan = (degree, cols, low, members, lines, share, norm_factor, 4.0 / math.sqrt(total_k))
    weights = (w_send, w_recv, w_basis, w_out)
    unmasked = force_step(
        features,
        atom_count,
        senders,
        edge_basis,
        jnp.cos(angles),
        jnp.sin(angles),
        weights,
        filter_rows,
        w_mix,
        plan,
    )
    live = jnp.arange(atom_rows, dtype=jnp.int32) < atom_count[0]
    return jnp.where(live[:, None], unmasked, 0.0)


def solution(mesh):
    placed = (
        P(("slab", "sub"), None),
        P(None, ("slab", "sub")),
        P(("slab", "sub")),
        P(),
        P(),
        P(),
        P(),
        P(),
        P(),
        P(),
        P(None, ("slab", "sub")),
        P(("slab", "sub")),
    )
    return jax.shard_map(
        per_device, mesh=mesh, in_specs=placed, out_specs=P(("slab", "sub"), None), check_vma=False
    )
```

```python
import math

import jax
import jax.numpy as jnp
from jax import lax
from jax.experimental import pallas as pl
from jax.experimental.pallas import tpu as pltpu
from jax.sharding import PartitionSpec as P

KMAX = 6
SIDE = 2 * KMAX + 1
PAIRS = 96
MIB = 1024 * 1024
CONTRACT_FIRST = (((0,), (0,)), ((), ()))


def fill_base(positions, base_cos, base_sin):
    rows = lax.broadcasted_iota(jnp.int32, (16, positions.shape[1]), 0).astype(jnp.float32)
    for axis in range(3):
        turns = (rows if axis == 0 else rows - KMAX) * positions[axis : axis + 1, :]
        angle = (turns - jnp.round(turns)) * math.pi
        square = angle * angle
        sine = jnp.full_like(angle, -1.0 / math.factorial(11))
        for n, sign in ((9, 1), (7, -1), (5, 1), (3, -1), (1, 1)):
            sine = sine * square + sign / math.factorial(n)
        sine = sine * angle
        cosine = jnp.full_like(angle, 1.0 / math.factorial(12))
        for n, sign in ((10, -1), (8, 1), (6, -1), (4, 1), (2, -1), (0, 1)):
            cosine = cosine * square + sign / math.factorial(n)
        base_cos[axis * 16 : axis * 16 + 16, :] = 1.0 - 2.0 * sine * sine
        base_sin[axis * 16 : axis * 16 + 16, :] = 2.0 * sine * cosine


def pick_filters(kgrid_ref, k_filter, first_row, share, filter_ref):
    total_k = kgrid_ref.shape[1]
    waves = [kgrid_ref[axis : axis + 1, :] for axis in range(3)]
    flip = jnp.where(waves[0] < 0, -1, 1)
    spot = (waves[2] * flip + KMAX) * PAIRS + waves[0] * flip * SIDE + waves[1] * flip + KMAX
    rows = first_row + lax.broadcasted_iota(jnp.int32, (share, total_k), 0)
    picks = jnp.where(rows == spot, 1.0, 0.0)
    summed = jnp.dot(
        picks, k_filter[...], precision=lax.Precision.HIGHEST, preferred_element_type=jnp.float32
    )
    filter_ref[:share, :] = summed
    filter_ref[share:, :] = summed


def fill_tables(base_cos, base_sin, masked_ref, table_ref, sums_ref, pair_cos, pair_sin):
    grid_rows = table_ref.shape[0] // 2
    channels = masked_ref.shape[1]
    atom_rows = masked_ref.shape[0]
    for a in range(KMAX + 1):
        cx, sx = base_cos[a : a + 1, :], base_sin[a : a + 1, :]
        cy, sy = base_cos[16 : 16 + SIDE, :], base_sin[16 : 16 + SIDE, :]
        pair_cos[a * SIDE : (a + 1) * SIDE, :] = cx * cy - sx * sy
        pair_sin[a * SIDE : (a + 1) * SIDE, :] = sx * cy + cx * sy
    used = (KMAX + 1) * SIDE
    pair_cos[used:, :] = jnp.zeros((PAIRS - used, atom_rows), jnp.float32)
    pair_sin[used:, :] = jnp.zeros((PAIRS - used, atom_rows), jnp.float32)

    def one_plane(q, carry):
        cz, sz = base_cos[pl.ds(32 + q, 1), :], base_sin[pl.ds(32 + q, 1), :]
        cosines = (pair_cos[...] * cz - pair_sin[...] * sz).astype(jnp.bfloat16)
        sines = (pair_sin[...] * cz + pair_cos[...] * sz).astype(jnp.bfloat16)
        at = pl.multiple_of(q * PAIRS, PAIRS)
        table_ref[pl.ds(at, PAIRS), :] = cosines
        table_ref[pl.ds(at + grid_rows, PAIRS), :] = sines
        sums_ref[pl.ds(at, PAIRS), :channels] = jnp.dot(
            cosines, masked_ref[...], preferred_element_type=jnp.float32
        ).astype(jnp.bfloat16).astype(jnp.bfloat16)
        sums_ref[pl.ds(at, PAIRS), channels:] = jnp.dot(
            sines, masked_ref[...], preferred_element_type=jnp.float32
        ).astype(jnp.bfloat16)
        return carry

    lax.fori_loop(0, SIDE, one_plane, 0)
    tail = grid_rows - SIDE * PAIRS
    if tail:
        for start in (SIDE * PAIRS, grid_rows + SIDE * PAIRS):
            table_ref[start : start + tail, :] = jnp.zeros((tail, atom_rows), jnp.bfloat16)
        sums_ref[SIDE * PAIRS :, :] = jnp.zeros((tail, 2 * channels), jnp.bfloat16)


def edge_loop(degree, snd_ref, pool, base, base_first, total, total_first):
    group = 4
    edges = group * degree
    count = snd_ref.shape[0] // edges
    sublane = lax.broadcasted_iota(jnp.int32, (8, pool.shape[1]), 0)
    masks = [sublane == k for k in range(8)]

    def gather(it):
        first = pl.multiple_of(it * edges, edges)
        parts = []
        for octet in range(edges // 8):
            start = first + octet * 8
            picked = pool[pl.ds(snd_ref[start], 8), :]
            for k in range(1, 8):
                picked = jnp.where(masks[k], pool[pl.ds(snd_ref[start + k], 8), :], picked)
            at = pl.multiple_of(base_first + first + octet * 8, 8)
            parts.append(picked + base[pl.ds(at, 8), :])
        return tuple(parts)

    def finish(it, halves):
        row = total_first + it * group
        for j in range(group):
            acc = None
            for half in halves[j * degree // 8 : (j + 1) * degree // 8]:
                hidden = (half + half * jnp.tanh(half)).astype(jnp.bfloat16).astype(jnp.float32)
                acc = hidden if acc is None else acc + hidden
            total[pl.ds(row + j, 1), :] = jnp.sum(acc, axis=0, keepdims=True)

    def one(it, halves):
        following = gather(it + 1)
        finish(it, halves)
        return following

    last = lax.fori_loop(0, count - 1, one, gather(0))
    finish(count - 1, last)


def edge_base(degree, basis_ref, w_basis, recv, base, start, count):
    atoms = 64
    edges = atoms * degree
    channels = recv.shape[1]

    def some(n, carry):
        first = pl.multiple_of(n * edges, edges)
        radial = lax.dot_general(
            basis_ref[:, pl.ds(pl.multiple_of(start * degree + first, edges), edges)],
            w_basis[...],
            CONTRACT_FIRST,
            preferred_element_type=jnp.float32,
        )
        rows = recv[pl.ds(pl.multiple_of(start + n * atoms, atoms), atoms), :]
        both = radial.reshape(atoms, degree, channels) + rows[:, None, :]
        base[pl.ds(first, edges), :] = 0.5 * both.reshape(edges, channels)
        return carry

    lax.fori_loop(0, count // atoms, some, 0)


def fused_kernel(
    plan,
    snd_ref,
    basis_ref,
    feat_ref,
    count_ref,
    positions,
    kgrid_ref,
    k_filter,
    w_send,
    w_recv,
    w_basis,
    w_out,
    w_mix,
    out_ref,
    base_cos,
    base_sin,
    filter_ref,
    strips,
    pool,
    masked,
    pair_cos,
    pair_sin,
    table,
    sums_ref,
    factor_ref,
    recv,
    base,
    total,
    in_plane,
    part,
    in_line,
    line_rows,
    plane_rows,
    send_a,
    recv_a,
    send_b,
    recv_b,
    send_c,
    recv_c,
    send_d,
    recv_d,
    send_x,
    recv_x,
    send_z,
    recv_z,
):
    degree, cols, low, members, lines, share, norm_factor, scale = plan
    block_rows, channels = feat_ref.shape
    slabs = low * lines
    home = 0 if cols == 2 else 1
    blocks = strips.shape[1]
    atoms = snd_ref.shape[0] // degree
    whole_base = base.shape[0] == block_rows * degree
    step = pl.program_id(0)
    slab, sub = lax.axis_index("slab"), lax.axis_index("sub")
    line = slab // low
    member = (slab % low) * cols + sub
    chunk = lines * share

    def plane_peer(r):
        peer = (member + r) % members
        return peer, {"slab": line * low + peer // cols, "sub": peer % cols}

    def line_peer(r):
        peer = (line + r) % lines
        return peer, {"slab": peer * low + slab % low, "sub": sub}

    def copy_a(r):
        peer, where = plane_peer(r)
        rows = pl.ds(pl.multiple_of(peer * chunk, 16), chunk)
        return pltpu.make_async_remote_copy(
            src_ref=sums_ref.at[rows],
            dst_ref=in_plane.at[r - 1],
            send_sem=send_a.at[r - 1],
            recv_sem=recv_a.at[r - 1],
            device_id=where,
            device_id_type=pl.DeviceIdType.MESH,
        )

    def copy_b(r):
        peer, where = line_peer(r)
        rows = pl.ds(pl.multiple_of(peer * share, 8), share)
        return pltpu.make_async_remote_copy(
            src_ref=part.at[rows],
            dst_ref=in_line.at[r - 1],
            send_sem=send_b.at[r - 1],
            recv_sem=recv_b.at[r - 1],
            device_id=where,
            device_id_type=pl.DeviceIdType.MESH,
        )

    def copy_c(r):
        peer, where = line_peer(r)
        return pltpu.make_async_remote_copy(
            src_ref=line_rows.at[line],
            dst_ref=line_rows.at[line],
            send_sem=send_c.at[r - 1],
            recv_sem=recv_c.at[r - 1],
            device_id=where,
            device_id_type=pl.DeviceIdType.MESH,
        )

    def copy_d(r):
        peer, where = plane_peer(r)
        return pltpu.make_async_remote_copy(
            src_ref=line_rows,
            dst_ref=plane_rows.at[member],
            send_sem=send_d.at[r - 1],
            recv_sem=recv_d.at[r - 1],
            device_id=where,
            device_id_type=pl.DeviceIdType.MESH,
        )

    def each(count, action):
        def one(r, carry):
            action(r)
            return carry

        lax.fori_loop(1, count, one, 0)

    sides = [(1, 1)] if cols == 2 else [(1, 0), (-1, 2)]

    def column_of(by):
        return {"slab": slab, "sub": (sub + by + cols) % cols}

    def slab_of(by):
        return {"slab": (slab + by + slabs) % slabs, "sub": sub}

    def copy_x(n):
        by, slot = sides[n]
        return pltpu.make_async_remote_copy(
            src_ref=strips.at[1, home],
            dst_ref=strips.at[1, slot],
            send_sem=send_x.at[n],
            recv_sem=recv_x.at[n],
            device_id=column_of(by),
            device_id_type=pl.DeviceIdType.MESH,
        )

    def copy_z(up, c):
        return pltpu.make_async_remote_copy(
            src_ref=strips.at[1, c],
            dst_ref=strips.at[0 if up else 2, c],
            send_sem=send_z.at[up * blocks + c],
            recv_sem=recv_z.at[up * blocks + c],
            device_id=slab_of(1 if up else -1),
            device_id_type=pl.DeviceIdType.MESH,
        )

    def spread(a, c):
        first = (a * blocks + c) * block_rows

        def some(n, carry):
            at = pl.multiple_of(n * 16, 16)
            rows = strips[a, c, pl.ds(at, 16), :].astype(jnp.float32)
            pool[pl.ds(pl.multiple_of(first + at + 8, 8), 16), :] = 0.5 * rows
            return carry

        lax.fori_loop(0, block_rows // 16, some, 0)

    def live(width):
        rows = lax.broadcasted_iota(jnp.int32, (block_rows, width), 0)
        return rows < count_ref[0]

    @pl.when(step == 0)
    def _():
        margin = jnp.zeros((8, channels), jnp.float32)
        pool[:8, :] = margin
        pool[pool.shape[0] - 8 :, :] = margin
        strips[1, home] = jnp.dot(
            feat_ref[...], w_send[...], preferred_element_type=jnp.float32
        ).astype(jnp.bfloat16)
        barrier = pltpu.get_barrier_semaphore()

        def greet(where):
            pl.semaphore_signal(
                barrier, inc=1, device_id=where, device_id_type=pl.DeviceIdType.MESH
            )

        each(members, lambda r: greet(plane_peer(r)[1]))
        each(lines, lambda r: greet(line_peer(r)[1]))
        for by, slot in sides:
            greet(column_of(by))
        greet(slab_of(1))
        greet(slab_of(-1))
        pl.semaphore_wait(barrier, members + lines + len(sides))
        for n in range(len(sides)):
            copy_x(n).start()
        for up in (1, 0):
            copy_z(up, home).start()
        masked[...] = jnp.where(live(channels), feat_ref[...].astype(jnp.float32), 0.0).astype(
            jnp.bfloat16
        )
        fill_base(positions, base_cos, base_sin)
        fill_tables(base_cos, base_sin, masked, table, sums_ref, pair_cos, pair_sin)
        for n, (by, slot) in enumerate(sides):
            copy_x(n).wait_recv()
            for up in (1, 0):
                copy_z(up, slot).start()
        pick_filters(kgrid_ref, k_filter, (member * lines + line) * share, share, filter_ref)
        recv[...] = jnp.dot(feat_ref[...], w_recv[...], preferred_element_type=jnp.float32)
        if whole_base:
            edge_base(degree, basis_ref, w_basis, recv, base, 0, block_rows)
        for c in range(blocks):
            spread(1, c)
        for c in [home] + [slot for by, slot in sides]:
            for up in (1, 0):
                copy_z(up, c).wait_recv()
                if c == sides[-1][1] and up == 0:
                    each(members, lambda r: copy_a(r).start())
                spread(0 if up else 2, c)

    @pl.when(step == 2)
    def _():
        each(members, lambda r: copy_a(r).wait_recv())
        part[...] = sums_ref[pl.ds(pl.multiple_of(member * chunk, 16), chunk), :].astype(jnp.float32)

        def add(r):
            part[...] += in_plane[r - 1].astype(jnp.float32)

        each(members, add)
        each(lines, lambda r: copy_b(r).start())

    @pl.when(step == 4)
    def _():
        each(lines, lambda r: copy_b(r).wait_recv())
        owned = part[pl.ds(pl.multiple_of(line * share, 8), share), :]
        for r in range(1, lines):
            owned = owned + in_line[r - 1]
        stacked = jnp.concatenate([owned[:, :channels], owned[:, channels:]], axis=0)
        scaled = stacked * norm_factor * filter_ref[...]
        line_rows[line] = jnp.dot(
            scaled,
            w_mix[...],
            precision=lax.Precision.HIGHEST,
            preferred_element_type=jnp.float32,
        ).astype(jnp.bfloat16)
        each(lines, lambda r: copy_c(r).start())

    @pl.when(step == 5)
    def _():
        each(lines, lambda r: copy_c(r).wait_recv())
        each(members, lambda r: copy_d(r).start())

    row = pl.multiple_of(step * atoms, atoms)
    if not whole_base:
        edge_base(degree, basis_ref, w_basis, recv, base, row, atoms)
    edge_loop(degree, snd_ref, pool, base, row * degree if whole_base else 0, total, row)

    @pl.when(step == pl.num_programs(0) - 1)
    def _():
        for n in range(len(sides)):
            copy_x(n).wait_send()
        for up in (1, 0):
            for c in range(blocks):
                copy_z(up, c).wait_send()
        each(members, lambda r: copy_a(r).wait_send())
        each(lines, lambda r: copy_b(r).wait_send())
        each(lines, lambda r: copy_c(r).wait_send())
        each(members, lambda r: copy_d(r).wait())
        plane_rows[member] = line_rows[...]
        grid_rows = factor_ref.shape[0] // 2

        def lay(n, carry):
            rows = plane_rows[n // lines, n % lines].astype(jnp.float32)
            factor_ref[pl.ds(pl.multiple_of(n * share, 8), share), :] = rows[:share]
            factor_ref[pl.ds(pl.multiple_of(grid_rows + n * share, 8), share), :] = rows[share:]
            return carry

        lax.fori_loop(0, members * lines, lay, 0)
        spread_t = lax.dot_general(
            factor_ref[...].astype(jnp.bfloat16),
            table[...],
            CONTRACT_FIRST,
            preferred_element_type=jnp.float32,
        )
        high = total[...].astype(jnp.bfloat16)
        low_part = (total[...] - high.astype(jnp.float32)).astype(jnp.bfloat16)
        aggregate = (
            jnp.dot(high, w_out[...], preferred_element_type=jnp.float32)
            + jnp.dot(low_part, w_out[...], preferred_element_type=jnp.float32)
        ) * (1.0 / math.sqrt(degree))
        out_ref[...] = aggregate + spread_t.T * scale


def whole(shape):
    return pl.BlockSpec(shape, lambda i: (0,) * len(shape), pipeline_mode=pl.Buffered(1))


def force_step(
    features, atom_count, senders, edge_basis, positions, kgrid, k_filter, weights, w_mix, plan
):
    degree, cols, low, members, lines, share, norm_factor, scale = plan
    atom_rows, channels = features.shape
    grid_rows = members * lines * share
    blocks = 2 if cols == 2 else 3
    step = 128
    base_atoms = atom_rows
    dma = pltpu.SemaphoreType.DMA
    f32, bf16 = jnp.float32, jnp.bfloat16
    return pl.pallas_call(
        lambda *refs: fused_kernel(plan, *refs),
        grid=(atom_rows // step,),
        in_specs=[
            pl.BlockSpec((step * degree,), lambda i: (i,), memory_space=pltpu.SMEM),
            whole(edge_basis.shape),
            whole(features.shape),
            pl.BlockSpec(memory_space=pltpu.SMEM),
            whole(positions.shape),
            whole(kgrid.shape),
            whole(k_filter.shape),
            *[whole(weight.shape) for weight in weights],
            whole(w_mix.shape),
        ],
        out_specs=whole((atom_rows, channels)),
        out_shape=jax.ShapeDtypeStruct((atom_rows, channels), f32),
        scratch_shapes=[
            pltpu.VMEM((48, atom_rows), f32),
            pltpu.VMEM((48, atom_rows), f32),
            pltpu.VMEM((2 * share, channels), f32),
            pltpu.VMEM((3, blocks, atom_rows, channels), bf16),
            pltpu.VMEM((3 * blocks * atom_rows + 16, channels), f32),
            pltpu.VMEM((atom_rows, channels), bf16),
            pltpu.VMEM((PAIRS, atom_rows), f32),
            pltpu.VMEM((PAIRS, atom_rows), f32),
            pltpu.VMEM((2 * grid_rows, atom_rows), bf16),
            pltpu.VMEM((grid_rows, 2 * channels), bf16),
            pltpu.VMEM((2 * grid_rows, channels), f32),
            pltpu.VMEM((atom_rows, channels), f32),
            pltpu.VMEM((base_atoms * degree, channels), f32),
            pltpu.VMEM((atom_rows, channels), f32),
            pltpu.VMEM((members - 1, lines * share, 2 * channels), bf16),
            pltpu.VMEM((lines * share, 2 * channels), f32),
            pltpu.VMEM((lines - 1, share, 2 * channels), f32),
            pltpu.VMEM((lines, 2 * share, channels), bf16),
            pltpu.VMEM((members, lines, 2 * share, channels), bf16),
            *[dma((members - 1,))] * 2,
            *[dma((lines - 1,))] * 4,
            *[dma((members - 1,))] * 2,
            *[dma((blocks - 1,))] * 2,
            *[dma((2 * blocks,))] * 2,
        ],
        compiler_params=pltpu.CompilerParams(
            vmem_limit_bytes=62 * MIB, collective_id=0, has_side_effects=True
        ),
        cost_estimate=pl.CostEstimate(
            flops=atom_rows * degree * channels * 200,
            bytes_accessed=atom_rows * degree * channels * 16,
            transcendentals=atom_rows * degree * channels,
        ),
        name="force_step",
    )(
        senders, edge_basis, features, atom_count, positions, kgrid, k_filter, *weights, w_mix
    )


def per_device(
    features,
    positions,
    atom_count,
    kgrid,
    k_filter,
    w_mix,
    w_recv,
    w_send,
    w_basis,
    w_out,
    edge_basis,
    senders,
):
    atom_rows, channels = features.shape
    degree = senders.shape[0] // atom_rows
    total_k = kgrid.shape[1]
    devices = lax.axis_size(("slab", "sub"))
    cols = lax.axis_size("sub")
    unit = devices * 8
    grid_rows = -(-SIDE * PAIRS // unit) * unit
    share = grid_rows // devices
    norm_factor = 1.0 / math.sqrt(atom_rows * devices)
    if cols == 2:
        block = senders // atom_rows
        slab_step = block // 3
        col_step = block - 3 * slab_step
        senders = (slab_step * 2 + (col_step != 1)) * atom_rows + (senders - block * atom_rows)

    senders = senders + (8 - jnp.arange(senders.shape[0], dtype=jnp.int32) % 8)

    low = 4
    lines = lax.axis_size("slab") // low
    members = low * cols
    plan = (degree, cols, low, members, lines, share, norm_factor, 4.0 / math.sqrt(total_k))
    weights = (w_send, w_recv, w_basis, w_out)
    unmasked = force_step(
        features,
        atom_count,
        senders,
        edge_basis,
        positions,
        kgrid,
        k_filter,
        weights,
        w_mix,
        plan,
    )
    live = jnp.arange(atom_rows, dtype=jnp.int32) < atom_count[0]
    return jnp.where(live[:, None], unmasked, 0.0)


def solution(mesh):
    placed = (
        P(("slab", "sub"), None),
        P(None, ("slab", "sub")),
        P(("slab", "sub")),
        P(),
        P(),
        P(),
        P(),
        P(),
        P(),
        P(),
        P(None, ("slab", "sub")),
        P(("slab", "sub")),
    )
    return jax.shard_map(
        per_device, mesh=mesh, in_specs=placed, out_specs=P(("slab", "sub"), None), check_vma=False
    )
```
